256 devices in a mesh: slab: 16 (over x, y), pencil: 16 (over z, core).
Axes of the slice: x: 4, y: 4, z: 8, core: 2. Of those that a mesh axis runs over, the one named last changes fastest.
Arguments:
- spec_vel: float32 [64, 1024, 2048], P('slab', None, 'pencil'), may hold values from -6 to 6
- shear_shift: int32 [64], P('slab'), may hold values from 0 to 1023
- patch_pos: int32 [16, 16, 3, 256], P('slab', 'pencil'), may hold values from 0 to 1008, as said below
- patch_count: int32 [16, 16], P('slab', 'pencil'), may hold values from 1 to 256, as said below
- interp_w: bfloat16 [16, 16, 64, 64, 256], P('slab', 'pencil'), may hold values from -0.75 to 0.75
- marker_vel: float32 [16, 16, 64, 256], P('slab', 'pencil'), may hold values from -6 to 6
Outputs:
- new_hat: float32 [64, 1024, 2048], P('slab', None, 'pencil')
- marker_force: float32 [16, 16, 64, 256], P('slab', 'pencil')
The draws below stay inside these ranges and needn't reach their ends.
Inputs may be any that keep to these rules, and one draw needn't show every extreme that they name: `patch_pos`: rows of a slot: first plane below 4, and at most 0 on the last slab; cell along the second dimension below 64; first cell along the third dimension at most 1008, reached on every device. `patch_count`: some device has all 256 slots live.
All inputs are finite; a program needn't handle non-finite values.
Results may differ from the reference program's by a relative error of at most 0.0036.
Values may be sent and summed in bfloat16 or wider, within the bound.
No kernel may reach another device: no remote copies, remote signals or barrier semaphores. Data moves between devices by JAX's collectives and lax.ppermute only.
A program may use at most 64 MiB of HBM per device.

```python
import math
import jax
import jax.numpy as jnp
from jax import lax

CX = 4
NY = 1024
NZ = 1024
PD = 4
PZ = 16
PM = 64
CAP = 256
PC = 64
NX = 64
CY = 64
N_SLAB = 16
N_PENCIL = 16


def draw_patch_pos(key, part):
    n_slab = NX // CX
    n_pencil = NY // CY
    keys_all = jax.random.split(jax.random.fold_in(key, 23), 4)
    slab_ids = jnp.arange(n_slab, dtype=jnp.int32)[:, None, None]
    highest = jnp.where(slab_ids == n_slab - 1, CX - PD, CX - 1)
    first_plane = jnp.minimum(jax.random.randint(keys_all[0], (n_slab, n_pencil, CAP), 0, CX), highest)
    across = jax.random.randint(keys_all[1], (n_slab, n_pencil, CAP), 0, CY)
    start_z = jax.random.randint(keys_all[2], (n_slab, n_pencil, CAP), 0, NZ - PZ + 1)
    chosen = jax.random.randint(keys_all[3], (n_slab, n_pencil, 1), 0, CAP)
    slot_ids = jnp.arange(CAP, dtype=jnp.int32)[None, None, :]
    start_z = jnp.where(slot_ids == chosen, NZ - PZ, start_z)
    return jnp.stack([first_plane, across, start_z], axis=2).astype(jnp.int32)


def draw_patch_count(key, part):
    n_slab = NX // CX
    n_pencil = NY // CY
    key_first, key_second = jax.random.split(jax.random.fold_in(key, 11))
    raw_draw = jax.random.randint(key_first, (n_slab * n_pencil,), 0, CAP + 1)
    counts = CAP // 8 + raw_draw * raw_draw // CAP * (CAP - CAP // 8) // CAP
    busiest = jax.random.randint(key_second, (), 0, n_slab * n_pencil)
    counts = jnp.where(jnp.arange(n_slab * n_pencil, dtype=jnp.int32) == busiest, CAP, counts)
    return jnp.maximum(counts, 1).reshape(n_slab, n_pencil).astype(jnp.int32)


def touch_ends(entries, own_key, low, top_value):
    spot = [jax.random.randint(jax.random.fold_in(own_key, axis), (), 0, length) for axis, length in enumerate(entries.shape)]
    longest = entries.shape.index(max(entries.shape))
    neighbour = spot[:longest] + [(spot[longest] + 1) % entries.shape[longest]] + spot[longest + 1:]
    return entries.at[tuple(spot)].set(low).at[tuple(neighbour)].set(top_value)


def levels(rng, shape, shards, smallest, top_value):
    level = 1.0
    for dim, blocks in shards:
        steps = jax.random.uniform(jax.random.fold_in(jax.random.fold_in(rng, 6), dim), (blocks,), jnp.float32, smallest / len(shards), top_value / len(shards))
        level = level * jnp.repeat(jnp.exp(steps), shape[dim] // blocks).reshape((-1,) + (1,) * (len(shape) - 1 - dim))
    return level


def centred(stream_key, shape, scale, limit, cuts=(), kind=jnp.bfloat16):
    result = scale * jax.random.normal(stream_key, shape, jnp.float32)
    if cuts:
        result = result * levels(stream_key, shape, cuts, -0.22, 0.18)
    return jnp.clip(result, -limit, limit).astype(kind)


def setup_inputs(seed: int = 0) -> dict:
    key_list = jax.random.split(jax.random.key(seed), 7)
    spec_vel = centred(key_list[0], (NX, NY, 2 * NZ), 1.0, 6.0, ((0, 16), (2, 16)), jnp.float32)
    shear_shift = touch_ends(jax.random.randint(key_list[1], (NX,), 0, NZ), jax.random.fold_in(key_list[1], 1), 0, NZ - 1).astype(jnp.int32)
    patch_pos = draw_patch_pos(jax.random.fold_in(key_list[6], 71), 0)
    patch_count = draw_patch_count(jax.random.fold_in(key_list[6], 71), 0)
    interp_w = centred(key_list[4], (N_SLAB, N_PENCIL, PM, PC, CAP), PC ** -0.5, 0.75, ((0, 16), (1, 16)))
    marker_vel = centred(key_list[5], (N_SLAB, N_PENCIL, PM, CAP), 1.0, 6.0, ((0, 16), (1, 16)), jnp.float32)
    return {"spec_vel": spec_vel, "shear_shift": shear_shift, "patch_pos": patch_pos, "patch_count": patch_count, "interp_w": interp_w, "marker_vel": marker_vel}


def dft_tables(length):
    steps_along = jnp.arange(length, dtype=jnp.int32)
    whole_turns = steps_along[:, None] * steps_along[None, :] % length
    angles = whole_turns.astype(jnp.float32) * (2.0 * math.pi / length)
    norming = 1.0 / math.sqrt(length)
    return ((jnp.cos(angles) * norming).astype(jnp.bfloat16), (jnp.sin(angles) * norming).astype(jnp.bfloat16))

def depth_table(length):
    cosine, sines = dft_tables(length)
    return jnp.stack([cosine, -sines], axis=1).reshape(2 * length, length)

def rotate(values):
    paired = values.reshape(values.shape[:-1] + (values.shape[-1] // 2, 2))
    return jnp.stack([-paired[..., 1], paired[..., 0]], axis=-1).reshape(values.shape)

def shear_phase(spectral, shifts, first_wave, length):
    wave_ids = first_wave + jnp.arange(spectral.shape[-1] // 2, dtype=jnp.int32)
    whole_turns = shifts[:, None] * wave_ids[None, :] % length
    angles = whole_turns.astype(jnp.float32) * (2.0 * math.pi / length)
    cosine = jnp.cos(angles)[:, None, :]
    sines = jnp.sin(angles)[:, None, :]
    paired = spectral.reshape(spectral.shape[:-1] + (spectral.shape[-1] // 2, 2))
    real_part = paired[..., 0]
    imag_part = paired[..., 1]
    turned = jnp.stack([real_part * cosine - imag_part * sines, real_part * sines + imag_part * cosine], axis=-1)
    return turned.reshape(spectral.shape)

def viscous_factor(row_count, first_wave, wave_count, length):
    across = jnp.arange(row_count, dtype=jnp.int32)
    along_z = first_wave + jnp.arange(wave_count, dtype=jnp.int32)
    across_norm = jnp.minimum(across, row_count - across).astype(jnp.float32) / (row_count // 2)
    along_norm = jnp.minimum(along_z, length - along_z).astype(jnp.float32) / (length // 2)
    factor = 1.0 / (1.0 + across_norm[:, None] ** 2 + along_norm[None, :] ** 2)
    return jnp.repeat(factor, 2, axis=1)

def along_rows(table_cos, table_sin, values, sign_flip):
    direct = jnp.einsum('yk,xkm->xym', table_cos.astype(jnp.float32), values.astype(jnp.float32), precision=lax.Precision.HIGHEST)
    second = jnp.einsum('yk,xkm->xym', table_sin.astype(jnp.float32), values.astype(jnp.float32), precision=lax.Precision.HIGHEST)
    return direct + sign_flip * rotate(second)

def reference(spec_vel, shear_shift, patch_pos, patch_count, interp_w, marker_vel):
    phased = shear_phase(spec_vel, shear_shift, 0, NZ)
    cosine_rows, sine_rows = dft_tables(NY)
    wave_table = depth_table(NZ)
    mixed_rows = along_rows(cosine_rows, sine_rows, phased.astype(jnp.bfloat16), 1.0).astype(jnp.bfloat16)
    velocity = jnp.dot(mixed_rows.reshape(NX * NY, 2 * NZ).astype(jnp.float32), wave_table.astype(jnp.float32), precision=lax.Precision.HIGHEST).reshape(NX, NY, NZ)
    cell_ids = jnp.arange(PD * PZ, dtype=jnp.int32)
    depth_step = cell_ids // PZ
    span_step = cell_ids % PZ
    pencil_rows = jnp.arange(N_PENCIL, dtype=jnp.int32) * CY
    flat_field = velocity.reshape(-1)
    slot_ids = jnp.arange(CAP, dtype=jnp.int32)

    def one_slab(slab_items):
        positions, live_count, weights, target, slab_index = slab_items
        planes_x = slab_index * CX + positions[:, 0]
        across = pencil_rows[:, None] + positions[:, 1]
        start_z = positions[:, 2]
        where_cells = ((planes_x[:, None, :] + depth_step[None, :, None]) * NY + across[:, None, :]) * NZ + start_z[:, None, :] + span_step[None, :, None]
        values = flat_field[where_cells]
        wide_weights = weights.astype(jnp.float32)
        interp = lax.optimization_barrier(jnp.sum(wide_weights * values[:, None, :, :], axis=2))
        live_slots = slot_ids[None, :] < live_count[:, None]
        forces = jnp.where(live_slots[:, None, :], target - interp, 0.0)
        spread = lax.optimization_barrier(jnp.sum(wide_weights * forces[:, :, None, :], axis=1))
        return (forces, where_cells, spread)
    forces, where_cells, spread = lax.map(one_slab, (patch_pos, patch_count, interp_w, marker_vel, jnp.arange(N_SLAB, dtype=jnp.int32)))
    forcing = jnp.zeros((NX * NY * NZ,), jnp.float32).at[where_cells.reshape(-1)].add(spread.reshape(-1)).reshape(NX, NY, NZ)
    source = forcing.astype(jnp.bfloat16)
    rows_hat = jnp.dot(source.reshape(NX * NY, NZ).astype(jnp.float32), wave_table.astype(jnp.float32).T, precision=lax.Precision.HIGHEST).reshape(NX, NY, 2 * NZ).astype(jnp.bfloat16)
    wave_part = along_rows(cosine_rows, sine_rows, rows_hat, -1.0)
    new_hat = viscous_factor(NY, 0, NZ, NZ)[None] * (phased + wave_part)
    return (new_hat, forces)
```

```python
import functools
import math

import jax
import jax.numpy as jnp
import ml_dtypes
import numpy as np
from jax import lax
from jax.experimental import pallas as pl
from jax.experimental.pallas import tpu as pltpu
from jax.sharding import PartitionSpec as P

PD = 4
PZ = 16
MIB = 1 << 20
F32 = jnp.float32
BF16 = jnp.bfloat16


def dft_tables(length):
    steps = np.arange(length, dtype=np.int64)
    turns = steps[:, None] * steps[None, :] % length
    angles = turns.astype(np.float32) * np.float32(2.0 * math.pi / length)
    norming = np.float32(1.0 / math.sqrt(length))
    return np.cos(angles) * norming, np.sin(angles) * norming


@functools.cache
def row_table(length):
    cosine, sines = dft_tables(length)
    return np.concatenate([cosine, sines], axis=1).astype(ml_dtypes.bfloat16)


@functools.cache
def depth_table(length):
    cosine, sines = dft_tables(length)
    merged = np.stack([cosine, -sines], axis=1).reshape(2 * length, length)
    return merged.astype(ml_dtypes.bfloat16)


def turn_cos_sin(turns):
    x = turns * math.pi
    x2 = x * x
    s = x * (
        1.0
        + x2
        * (
            -1.0 / 6
            + x2
            * (1.0 / 120 + x2 * (-1.0 / 5040 + x2 * (1.0 / 362880 + x2 * (-1.0 / 39916800))))
        )
    )
    c = 1.0 + x2 * (
        -0.5
        + x2
        * (1.0 / 24 + x2 * (-1.0 / 720 + x2 * (1.0 / 40320 + x2 * (-1.0 / 3628800))))
    )
    return 1.0 - 2.0 * s * s, 2.0 * s * c


def wave_turns(product, length):
    half = length // 2
    return (((product + half) & (length - 1)) - half).astype(F32) * (1.0 / length)


def rotate(values):
    width = values.shape[-1]
    lane = lax.broadcasted_iota(jnp.int32, values.shape, values.ndim - 1)
    axis = values.ndim - 1
    ahead = pltpu.roll(values, width - 1, axis)
    behind = pltpu.roll(values, 1, axis)
    return jnp.where(lane % 2 == 0, -ahead, behind)


def plane_phase(shift, first_wave, width, length):
    lane = lax.broadcasted_iota(jnp.int32, (1, width), 1)
    return turn_cos_sin(wave_turns((first_wave + lane // 2) * shift, length))


def forward_body(length, scal, spec, table, out, basis):
    planes, rows, width = spec.shape
    step = pl.program_id(0)

    @pl.when(step == 0)
    def _():
        for x in range(planes):
            cosine, sines = plane_phase(scal[1 + x], scal[0], width, length)
            values = spec[x]
            turned = rotate(values)
            lanes = pl.ds(x * width, width)
            basis[pl.ds(0, rows), lanes] = (values * cosine + turned * sines).astype(BF16)
            basis[pl.ds(rows, rows), lanes] = (turned * cosine - values * sines).astype(BF16)

    mixed = jnp.dot(table[...], basis[...], preferred_element_type=F32).astype(BF16)
    dests, _, own, _ = out.shape
    for d in range(dests):
        for x in range(planes):
            out[d, x] = mixed[d * own : (d + 1) * own, x * width : (x + 1) * width]


def forward_rows(scal, spec, table, own, length):
    planes, rows, width = spec.shape
    steps = 4
    tile = rows // steps
    return pl.pallas_call(
        functools.partial(forward_body, length),
        grid=(steps,),
        in_specs=[
            pl.BlockSpec(memory_space=pltpu.SMEM),
            pl.BlockSpec((planes, rows, width), lambda i: (0, 0, 0)),
            pl.BlockSpec((tile, 2 * rows), lambda i: (i, 0)),
        ],
        out_specs=pl.BlockSpec((tile // own, planes, own, width), lambda i: (i, 0, 0, 0)),
        out_shape=jax.ShapeDtypeStruct((rows // own, planes, own, width), BF16),
        scratch_shapes=[pltpu.VMEM((2 * rows, planes * width), BF16)],
        compiler_params=pltpu.CompilerParams(vmem_limit_bytes=40 * MIB),
        cost_estimate=pl.CostEstimate(
            flops=4 * rows * rows * planes * width,
            bytes_accessed=4 * planes * rows * width + 4 * rows * rows + 2 * planes * rows * width,
            transcendentals=0,
        ),
        name="forward_rows",
    )(scal, spec, table)


def cells_body(slots, pos, coefs, table, own_out, above_out, field, own_cells, above_cells):
    step = pl.program_id(0)
    last = pl.num_programs(0) - 1
    sources, rows, width = coefs.shape
    span = rows // PD

    @pl.when(step == 0)
    def _():
        field[:, pl.ds(rows, rows), :] = jnp.zeros((field.shape[0], rows, 128), F32)
        field[field.shape[0] - 1, pl.ds(0, rows), :] = jnp.zeros((rows, 128), F32)

    left = jnp.concatenate([coefs[j] for j in range(sources)], axis=1)
    velocity = jnp.dot(left, table[...], preferred_element_type=F32)
    parts = velocity.shape[1] // 128
    for j in range(parts):
        field[parts * step + j, pl.ds(0, rows), :] = velocity[:, j * 128 : (j + 1) * 128]

    @pl.when(step == last)
    def _():
        lane = lax.broadcasted_iota(jnp.int32, (8, 128), 1)

        def take(p, base, offset, into):
            first = pos[base + p]
            across = pos[base + slots + p]
            start = pos[base + 2 * slots + p]
            tile = start // 128
            off = start % 128
            near = field[tile, pl.ds(across, 8, stride=span), :]
            far = field[tile + 1, pl.ds(across, 8, stride=span), :]
            both = jnp.where(lane >= off, near, far)
            both = pltpu.roll(both, 128 - off, 1)
            both = pltpu.roll(both, (offset - first) % 8, 0)
            into[pl.ds(pl.multiple_of(p * 8, 8), 8), :] = both

        def body(i, carry):
            for u in range(8):
                take(i * 8 + u, 0, 8, own_cells)
                take(i * 8 + u, 3 * slots, 4, above_cells)
            return carry

        lax.fori_loop(0, slots // 8, body, 0)
        wide = lax.broadcasted_iota(jnp.int32, (slots, 128), 1) < PZ
        total = jnp.zeros((slots, 128), F32)
        for a in range(PD):
            part = jnp.where(wide, own_cells[pl.ds(a, slots, stride=8), :], 0.0)
            total += part if a == 0 else pltpu.roll(part, a * PZ, 1)
        for a in range(1, PD):
            part = jnp.where(wide, above_cells[pl.ds(a, slots, stride=8), :], 0.0)
            total += pltpu.roll(part, PD * PZ + a * PZ, 1)
        turned = total.T
        own_out[...] = turned[: PD * PZ]
        above_out[...] = turned[PD * PZ + PZ :]


def patch_cells(pos, coefs, table, slots):
    sources, rows, width = coefs.shape
    length = table.shape[1]
    steps = 4
    tile = length // steps
    return pl.pallas_call(
        functools.partial(cells_body, slots),
        grid=(steps,),
        in_specs=[
            pl.BlockSpec(memory_space=pltpu.SMEM),
            pl.BlockSpec((sources, rows, width), lambda i: (0, 0, 0)),
            pl.BlockSpec((sources * width, tile), lambda i: (0, i)),
        ],
        out_specs=[
            pl.BlockSpec((PD * PZ, slots), lambda i: (0, 0)),
            pl.BlockSpec(((PD - 1) * PZ, slots), lambda i: (0, 0)),
        ],
        out_shape=[
            jax.ShapeDtypeStruct((PD * PZ, slots), F32),
            jax.ShapeDtypeStruct(((PD - 1) * PZ, slots), F32),
        ],
        scratch_shapes=[
            pltpu.VMEM((length // 128 + 1, 2 * rows, 128), F32),
            pltpu.VMEM((slots * 8, 128), F32),
            pltpu.VMEM((slots * 8, 128), F32),
        ],
        compiler_params=pltpu.CompilerParams(vmem_limit_bytes=40 * MIB),
        name="patch_cells",
    )(pos, coefs, table)


def force_body(count, weights, own, above, target, forces, own_out, up_out, values, spread):
    step = pl.program_id(0)
    markers, cells, slots = weights.shape

    @pl.when(step == 0)
    def _():
        values[pl.ds(0, PZ), :] = own[pl.ds(0, PZ), :]
        values[pl.ds(PZ, cells - PZ), :] = own[pl.ds(PZ, cells - PZ), :] + above[...]
        spread[...] = jnp.zeros((cells, slots), F32)

    live = lax.broadcasted_iota(jnp.int32, (1, slots), 1) < count[0]
    held = values[...]
    total = spread[...]
    for m in range(markers):
        wide = weights[m].astype(F32)
        interp = jnp.sum(wide * held, axis=0, keepdims=True)
        force = jnp.where(live, target[pl.ds(m, 1), :] - interp, 0.0)
        forces[pl.ds(m, 1), :] = force
        total = total + wide * force
    spread[...] = total

    @pl.when(step == pl.num_programs(0) - 1)
    def _():
        own_out[...] = total.astype(BF16)
        up_out[...] = total[PZ:].astype(BF16)


def marker_forces(count, weights, own, above, target):
    markers, cells, slots = weights.shape
    steps = 4
    tile = markers // steps
    whole = lambda i: (0, 0)
    return pl.pallas_call(
        force_body,
        grid=(steps,),
        in_specs=[
            pl.BlockSpec(memory_space=pltpu.SMEM),
            pl.BlockSpec((tile, cells, slots), lambda i: (i, 0, 0)),
            pl.BlockSpec((cells, slots), whole),
            pl.BlockSpec((cells - PZ, slots), whole),
            pl.BlockSpec((tile, slots), lambda i: (i, 0)),
        ],
        out_specs=[
            pl.BlockSpec((tile, slots), lambda i: (i, 0)),
            pl.BlockSpec((cells, slots), whole),
            pl.BlockSpec((cells - PZ, slots), whole),
        ],
        out_shape=[
            jax.ShapeDtypeStruct((markers, slots), F32),
            jax.ShapeDtypeStruct((cells, slots), BF16),
            jax.ShapeDtypeStruct((cells - PZ, slots), BF16),
        ],
        scratch_shapes=[pltpu.VMEM((cells, slots), F32), pltpu.VMEM((cells, slots), F32)],
        compiler_params=pltpu.CompilerParams(vmem_limit_bytes=32 * MIB),
        name="marker_forces",
    )(count, weights, own, above, target)


def spread_table(first_wave, width, length):
    row = jnp.arange(2 * width, dtype=jnp.int32)[:, None]
    cell = jnp.arange(PZ, dtype=jnp.int32)[None, :]
    wave = first_wave + (row % width) // 2
    angles = (wave * cell % length).astype(F32) * (2.0 * math.pi / length)
    norming = 1.0 / math.sqrt(length)
    cosine = jnp.cos(angles) * norming
    sines = jnp.sin(angles) * norming
    odd = row % 2 == 1
    straight = jnp.where(odd, -sines, cosine)
    quarter = jnp.where(odd, -cosine, -sines)
    entry = jnp.where(row < width, straight, quarter)
    high = entry.astype(BF16)
    low = (entry - high.astype(F32)).astype(BF16)
    blocks = 2 * PD - 1
    eye = jnp.eye(blocks, dtype=BF16)
    halves = [
        (eye[:, None, :, None] * part[None, :, None, :]).reshape(blocks * 2 * width, blocks * PZ)
        for part in (high, low)
    ]
    return jnp.concatenate(halves, axis=1)


def back_body(length, merge_steps, scal, spread, meta, turn, table, spec, out, basis):
    step = pl.program_id(0)
    planes, tile, width = out.shape
    rows = basis.shape[0] // 2
    group, _, slots = spread.shape
    own = rows // (group * merge_steps)

    @pl.when(step < merge_steps)
    def _():
        wave = scal[0] + lax.broadcasted_iota(jnp.int32, (width, 1), 0) // 2
        place = lax.broadcasted_iota(jnp.int32, (planes * own, slots), 0)
        for g in range(group):
            half = spread[g]
            doubled = jnp.concatenate([half, half], axis=0)
            sums = [jnp.zeros((own, width), F32) for _ in range(planes)]
            for side in range(2):
                start = meta[g, pl.ds(2 * side, 1), :]
                key = meta[g, pl.ds(2 * side + 1, 1), :]
                cosine, sines = turn_cos_sin(wave_turns(wave * start, length))
                hot = jnp.where(place == key, 1.0, 0.0).astype(BF16)
                depths = range(PD) if side == 0 else range(1, PD)
                for a in depths:
                    block = a if side == 0 else PD + a - 1
                    flat = jnp.dot(
                        turn[pl.ds(block * 2 * width, 2 * width), :],
                        doubled,
                        preferred_element_type=F32,
                    )
                    turned = (flat[:width] * cosine + flat[width:] * sines).astype(BF16)
                    if side == 0:
                        begin, count = 0, planes - a
                    else:
                        begin, count = PD - a, a
                    landed = lax.dot_general(
                        hot[begin * own : (begin + count) * own],
                        turned,
                        (((1,), (1,)), ((), ())),
                        preferred_element_type=F32,
                    )
                    for j in range(count):
                        x = begin + j + a - (0 if side == 0 else PD)
                        sums[x] = sums[x] + landed[j * own : (j + 1) * own]
            base = pl.multiple_of((step * group + g) * own, own)
            for x in range(planes):
                kept = sums[x].astype(BF16).astype(F32)
                lanes = pl.ds(x * width, width)
                basis[pl.ds(base, own), lanes] = kept.astype(BF16)
                basis[pl.ds(rows + base, own), lanes] = (-rotate(kept)).astype(BF16)

    @pl.when(step >= merge_steps)
    def _():
        mixed = jnp.dot(table[...], basis[...], preferred_element_type=F32)
        across = (step - merge_steps) * tile + lax.broadcasted_iota(jnp.int32, (tile, width), 0)
        along = scal[0] + lax.broadcasted_iota(jnp.int32, (tile, width), 1) // 2
        across_norm = jnp.minimum(across, rows - across).astype(F32) * (2.0 / rows)
        along_norm = jnp.minimum(along, length - along).astype(F32) * (2.0 / length)
        factor = 1.0 / (1.0 + across_norm * across_norm + along_norm * along_norm)
        for x in range(planes):
            cosine, sines = plane_phase(scal[1 + x], scal[0], width, length)
            values = spec[x]
            phased = values * cosine + rotate(values) * sines
            out[x] = factor * (phased + mixed[:, x * width : (x + 1) * width])


def back_rows(scal, spread, meta, turn, table, spec, length):
    planes, rows, width = spec.shape
    sources, cells, slots = spread.shape
    merge_steps = 4
    group = sources // merge_steps
    row_steps = 4
    tile = rows // row_steps
    merging = lambda i: (jnp.minimum(i, merge_steps - 1), 0, 0)
    later = lambda i: jnp.maximum(i - merge_steps, 0)
    return pl.pallas_call(
        functools.partial(back_body, length, merge_steps),
        grid=(merge_steps + row_steps,),
        in_specs=[
            pl.BlockSpec(memory_space=pltpu.SMEM),
            pl.BlockSpec((group, cells, slots), merging),
            pl.BlockSpec((group,) + meta.shape[1:], merging),
            pl.BlockSpec(turn.shape, lambda i: (0, 0)),
            pl.BlockSpec((tile, 2 * rows), lambda i: (later(i), 0)),
            pl.BlockSpec((planes, tile, width), lambda i: (0, later(i), 0)),
        ],
        out_specs=pl.BlockSpec((planes, tile, width), lambda i: (0, later(i), 0)),
        out_shape=jax.ShapeDtypeStruct((planes, rows, width), F32),
        scratch_shapes=[pltpu.VMEM((2 * rows, planes * width), BF16)],
        compiler_params=pltpu.CompilerParams(vmem_limit_bytes=48 * MIB),
        name="back_rows",
    )(scal, spread, meta, turn, table, spec)


def one_slab_on(value, by):
    size = lax.axis_size("slab")
    return lax.ppermute(value, "slab", [(i, i + by) for i in range(size) if 0 <= i + by < size])


def shards(spec_vel, shear_shift, patch_pos, patch_count, interp_w, marker_vel):
    planes, rows, width = spec_vel.shape
    pencils = lax.axis_size("pencil")
    own = rows // pencils
    length = width // 2 * pencils
    slots = patch_pos.shape[-1]
    first_wave = (lax.axis_index("pencil") * (width // 2)).astype(jnp.int32)
    scal = jnp.concatenate([first_wave[None], shear_shift])
    table = jnp.asarray(row_table(rows))

    positions = patch_pos[0, 0]
    behind = one_slab_on(positions, 1)
    coefs = forward_rows(scal, spec_vel, table, own, length)
    coefs = coefs.reshape(pencils, planes * own, width)
    here = lax.all_to_all(coefs, "pencil", split_axis=0, concat_axis=0, tiled=True)
    notes = jnp.stack(
        [
            positions[2],
            positions[0] * own + positions[1],
            behind[2],
            behind[0] * own + behind[1],
        ]
    )
    notes = jnp.concatenate([notes, jnp.zeros_like(notes)])[None]
    notes, _ = lax.optimization_barrier((notes, coefs))
    meta = lax.all_gather(notes, "pencil", axis=0, tiled=True)
    turn = spread_table(first_wave, width, length)

    flat_pos = jnp.concatenate([positions.reshape(-1), behind.reshape(-1)])
    values, above = patch_cells(flat_pos, here, jnp.asarray(depth_table(length)), slots)
    from_above = one_slab_on(above, -1)
    forces, spread, upward = marker_forces(
        patch_count[0], interp_w[0, 0], values, from_above, marker_vel[0, 0]
    )
    from_below = one_slab_on(upward, 1)
    message = jnp.concatenate([spread, from_below])[None]
    gathered = lax.all_gather(message, "pencil", axis=0, tiled=True)
    new_hat = back_rows(scal, gathered, meta, turn, table, spec_vel, length)
    return (new_hat, forces[None, None])


def solution(mesh):
    placed = (
        P("slab", None, "pencil"),
        P("slab"),
        P("slab", "pencil", None, None),
        P("slab", "pencil"),
        P("slab", "pencil", None, None, None),
        P("slab", "pencil", None, None),
    )
    return jax.shard_map(
        shards,
        mesh=mesh,
        in_specs=placed,
        out_specs=(P("slab", None, "pencil"), P("slab", "pencil", None, None)),
        check_vma=False,
    )
```

```python
import functools
import math

import jax
import jax.numpy as jnp
import ml_dtypes
import numpy as np
from jax import lax
from jax.experimental import pallas as pl
from jax.experimental.pallas import tpu as pltpu
from jax.sharding import PartitionSpec as P

PD = 4
PZ = 16
MIB = 1 << 20
VMEM_MIB = 56
PITCH = 9
FIELD_TILES = 9
FIELD_PLANES = 15
F32 = jnp.float32
BF16 = jnp.bfloat16


def dft_tables(length):
    steps = np.arange(length, dtype=np.int64)
    turns = steps[:, None] * steps[None, :] % length
    angles = turns.astype(np.float32) * np.float32(2.0 * math.pi / length)
    norming = np.float32(1.0 / math.sqrt(length))
    return np.cos(angles) * norming, np.sin(angles) * norming


@functools.cache
def row_table(length):
    cosine, sines = dft_tables(length)
    return np.concatenate([cosine, sines], axis=1).astype(ml_dtypes.bfloat16)


@functools.cache
def depth_table(length):
    cosine, sines = dft_tables(length)
    merged = np.stack([cosine, -sines], axis=1).reshape(2 * length, length)
    return merged.astype(ml_dtypes.bfloat16)


def turn_cos_sin(turns):
    x = turns * math.pi
    x2 = x * x
    s = x * (
        1.0
        + x2
        * (
            -1.0 / 6
            + x2
            * (1.0 / 120 + x2 * (-1.0 / 5040 + x2 * (1.0 / 362880 + x2 * (-1.0 / 39916800))))
        )
    )
    c = 1.0 + x2 * (
        -0.5
        + x2
        * (1.0 / 24 + x2 * (-1.0 / 720 + x2 * (1.0 / 40320 + x2 * (-1.0 / 3628800))))
    )
    return 1.0 - 2.0 * s * s, 2.0 * s * c


def wave_turns(product, length):
    half = length // 2
    return (((product + half) & (length - 1)) - half).astype(F32) * (1.0 / length)


def rotate(values):
    width = values.shape[-1]
    lane = lax.broadcasted_iota(jnp.int32, values.shape, values.ndim - 1)
    axis = values.ndim - 1
    ahead = pltpu.roll(values, width - 1, axis)
    behind = pltpu.roll(values, 1, axis)
    return jnp.where(lane % 2 == 0, -ahead, behind)


def plane_phase(shift, first_wave, width, length):
    lane = lax.broadcasted_iota(jnp.int32, (1, width), 1)
    return turn_cos_sin(wave_turns((first_wave + lane // 2) * shift, length))


def forward_body(length, prep_steps, scal, spec, table, out, basis):
    group, rows, width = spec.shape
    planes = group * prep_steps
    step = pl.program_id(0)
    for part in range(prep_steps):

        @pl.when(step == part)
        def _():
            for g in range(group):
                x = part * group + g
                cosine, sines = plane_phase(scal[1 + x], scal[0], width, length)
                values = spec[g]
                turned = rotate(values)
                lanes = pl.ds(x * width, width)
                basis[pl.ds(0, rows), lanes] = (values * cosine + turned * sines).astype(BF16)
                basis[pl.ds(rows, rows), lanes] = (turned * cosine - values * sines).astype(BF16)

    @pl.when(step >= prep_steps)
    def _():
        mixed = jnp.dot(table[...], basis[...], preferred_element_type=F32).astype(BF16)
        dests, _, own, _ = out.shape
        for d in range(dests):
            for x in range(planes):
                out[d, x] = mixed[d * own : (d + 1) * own, x * width : (x + 1) * width]


def forward_rows(scal, spec, table, own, length, prep_steps=2, row_steps=2):
    planes, rows, width = spec.shape
    tile = rows // row_steps
    later = lambda i: jnp.maximum(i - prep_steps, 0)
    return pl.pallas_call(
        functools.partial(forward_body, length, prep_steps),
        grid=(prep_steps + row_steps,),
        in_specs=[
            pl.BlockSpec(memory_space=pltpu.SMEM),
            pl.BlockSpec(
                (planes // prep_steps, rows, width),
                lambda i: (jnp.minimum(i, prep_steps - 1), 0, 0),
            ),
            pl.BlockSpec((tile, 2 * rows), lambda i: (later(i), 0)),
        ],
        out_specs=pl.BlockSpec((tile // own, planes, own, width), lambda i: (later(i), 0, 0, 0)),
        out_shape=jax.ShapeDtypeStruct((rows // own, planes, own, width), BF16),
        scratch_shapes=[pltpu.VMEM((2 * rows, planes * width), BF16)],
        compiler_params=pltpu.CompilerParams(vmem_limit_bytes=VMEM_MIB * MIB),
        cost_estimate=pl.CostEstimate(
            flops=4 * rows * rows * planes * width,
            bytes_accessed=4 * planes * rows * width + 4 * rows * rows + 2 * planes * rows * width,
            transcendentals=0,
        ),
        name="forward_rows",
    )(scal, spec, table)


def take_cells(spots, field, into, base, slots):
    lane = lax.broadcasted_iota(jnp.int32, (8, 128), 1)
    pitch = field.shape[0] // FIELD_TILES
    span = pitch // FIELD_PLANES
    batch = 16

    def body(i, carry):
        found = []
        for u in range(batch):
            spot = spots[base + i * batch + u]
            off = spots[base + slots + i * batch + u]
            near = field[pl.ds(spot, 8, stride=span), :]
            far = field[pl.ds(spot + pitch, 8, stride=span), :]
            found.append(pltpu.roll(jnp.where(lane >= off, near, far), 128 - off, 1))
        for u in range(batch):
            into[pl.ds((i * batch + u) * PITCH, 8), :] = found[u]
        return carry

    lax.fori_loop(0, slots // batch, body, 0)


def cells_first(into, slots):
    wide = lax.broadcasted_iota(jnp.int32, (slots, 128), 1) < PZ
    total = jnp.where(wide, into[pl.ds(0, slots, stride=PITCH), :], 0.0)
    for a in range(1, PD):
        part = jnp.where(wide, into[pl.ds(a, slots, stride=PITCH), :], 0.0)
        total += pltpu.roll(part, a * PZ, 1)
    return total.T


def above_body(slots, pos, coefs, table, field, above_out, into):
    step = pl.program_id(0)
    sources, rows, width = coefs.shape
    own = rows // PD
    span = own + 1
    pitch = FIELD_PLANES * span

    @pl.when(step == 0)
    def _():
        blank = jnp.zeros((PD * span, 128), F32)
        for t in range(FIELD_TILES):
            field[pl.ds(t * pitch, PD * span), :] = blank
            field[pl.ds(t * pitch + 2 * PD * span, (PD - 1) * span), :] = blank[span:]
        field[pl.ds((FIELD_TILES - 1) * pitch + PD * span, PD * span), :] = blank

    left = jnp.concatenate([coefs[j] for j in range(sources)], axis=1)
    velocity = jnp.dot(left, table[...], preferred_element_type=F32)
    parts = velocity.shape[1] // 128
    for j in range(parts):
        for x in range(PD):
            start = (parts * step + j) * pitch + (PD + x) * span
            field[pl.ds(start, own), :] = velocity[
                x * own : (x + 1) * own, j * 128 : (j + 1) * 128
            ]

    @pl.when(step == pl.num_programs(0) - 1)
    def _():
        take_cells(pos, field, into, 2 * slots, slots)
        above_out[...] = cells_first(into, slots)[PZ : PD * PZ]


def patch_spots(positions, behind, own):
    parts = []
    for held, lift in ((positions, PD), (behind, 0)):
        tile = held[2] // 128
        parts.append(
            (tile * FIELD_PLANES + held[0] + lift) * (own + 1) + held[1]
        )
        parts.append(held[2] % 128)
    return jnp.concatenate(parts)


def own_body(slots, pos, field, own_out, into):
    take_cells(pos, field, into, 0, slots)
    own_out[...] = cells_first(into, slots)[: PD * PZ]


def above_cells(pos, coefs, table, slots, steps=2):
    sources, rows, width = coefs.shape
    length = table.shape[1]
    span = rows // PD + 1
    tile = length // steps
    field_shape = (FIELD_TILES * FIELD_PLANES * span, 128)
    return pl.pallas_call(
        functools.partial(above_body, slots),
        grid=(steps,),
        in_specs=[
            pl.BlockSpec(memory_space=pltpu.SMEM),
            pl.BlockSpec((sources, rows, width), lambda i: (0, 0, 0)),
            pl.BlockSpec((sources * width, tile), lambda i: (0, i)),
        ],
        out_specs=[
            pl.BlockSpec(field_shape, lambda i: (0, 0)),
            pl.BlockSpec(((PD - 1) * PZ, slots), lambda i: (0, 0)),
        ],
        out_shape=[
            jax.ShapeDtypeStruct(field_shape, F32),
            jax.ShapeDtypeStruct(((PD - 1) * PZ, slots), F32),
        ],
        scratch_shapes=[pltpu.VMEM((slots * PITCH, 128), F32)],
        compiler_params=pltpu.CompilerParams(vmem_limit_bytes=VMEM_MIB * MIB),
        name="above_cells",
    )(pos, coefs, table)


def own_cells(pos, field, slots):
    return pl.pallas_call(
        functools.partial(own_body, slots),
        in_specs=[
            pl.BlockSpec(memory_space=pltpu.SMEM),
            pl.BlockSpec(memory_space=pltpu.VMEM),
        ],
        out_specs=pl.BlockSpec(memory_space=pltpu.VMEM),
        out_shape=jax.ShapeDtypeStruct((PD * PZ, slots), F32),
        scratch_shapes=[pltpu.VMEM((slots * PITCH, 128), F32)],
        compiler_params=pltpu.CompilerParams(vmem_limit_bytes=48 * MIB),
        name="own_cells",
    )(pos, field)


def force_body(count, weights, own, above, target, forces, own_out, up_out, values, spread):
    step = pl.program_id(0)
    markers, cells, slots = weights.shape

    @pl.when(step == 0)
    def _():
        values[pl.ds(0, PZ), :] = own[pl.ds(0, PZ), :]
        values[pl.ds(PZ, cells - PZ), :] = own[pl.ds(PZ, cells - PZ), :] + above[...]
        spread[...] = jnp.zeros((cells, slots), F32)

    live = lax.broadcasted_iota(jnp.int32, (1, slots), 1) < count[0]
    held = values[...]
    total = spread[...]
    for m in range(markers):
        wide = weights[m].astype(F32)
        interp = jnp.sum(wide * held, axis=0, keepdims=True)
        force = jnp.where(live, target[pl.ds(m, 1), :] - interp, 0.0)
        forces[pl.ds(m, 1), :] = force
        total = total + wide * force
    spread[...] = total

    @pl.when(step == pl.num_programs(0) - 1)
    def _():
        own_out[...] = total.astype(BF16)
        up_out[...] = total[PZ:].astype(BF16)


def marker_forces(count, weights, own, above, target):
    markers, cells, slots = weights.shape
    steps = 4
    tile = markers // steps
    whole = lambda i: (0, 0)
    return pl.pallas_call(
        force_body,
        grid=(steps,),
        in_specs=[
            pl.BlockSpec(memory_space=pltpu.SMEM),
            pl.BlockSpec((tile, cells, slots), lambda i: (i, 0, 0)),
            pl.BlockSpec((cells, slots), whole),
            pl.BlockSpec((cells - PZ, slots), whole),
            pl.BlockSpec((tile, slots), lambda i: (i, 0)),
        ],
        out_specs=[
            pl.BlockSpec((tile, slots), lambda i: (i, 0)),
            pl.BlockSpec((cells, slots), whole),
            pl.BlockSpec((cells - PZ, slots), whole),
        ],
        out_shape=[
            jax.ShapeDtypeStruct((markers, slots), F32),
            jax.ShapeDtypeStruct((cells, slots), BF16),
            jax.ShapeDtypeStruct((cells - PZ, slots), BF16),
        ],
        scratch_shapes=[pltpu.VMEM((cells, slots), F32), pltpu.VMEM((cells, slots), F32)],
        compiler_params=pltpu.CompilerParams(vmem_limit_bytes=32 * MIB),
        name="marker_forces",
    )(count, weights, own, above, target)


def spread_table(first_wave, width, length):
    half = width // 2
    row = jnp.arange(width, dtype=jnp.int32)[:, None]
    cell = jnp.arange(PZ, dtype=jnp.int32)[None, :]
    wave = first_wave + row % half
    cosine, sines = turn_cos_sin(wave_turns(wave * cell, length))
    entry = jnp.where(row < half, cosine, -sines) * (1.0 / math.sqrt(length))
    high = entry.astype(BF16)
    low = (entry - high.astype(F32)).astype(BF16)
    blocks = 2 * PD - 1
    eye = jnp.eye(blocks, dtype=BF16)
    halves = [
        (eye[:, None, :, None] * part[None, :, None, :]).reshape(blocks * width, blocks * PZ)
        for part in (high, low)
    ]
    return jnp.concatenate(halves, axis=1)


def lane_table(width):
    half = width // 2
    table = np.zeros((width, 2 * width), np.float32)
    for k in range(half):
        table[k, 2 * k] = 1.0
        table[half + k, 2 * k + 1] = 1.0
        table[half + k, width + 2 * k] = 1.0
        table[k, width + 2 * k + 1] = -1.0
    return table.astype(ml_dtypes.bfloat16)


def merge_sources(length, first_wave, parts, turn, own, planes, width):
    half = width // 2
    cells = (2 * PD - 1) * PZ
    slots = parts[0].shape[1]
    wave = first_wave + lax.broadcasted_iota(jnp.int32, (half, 1), 0)
    place = lax.broadcasted_iota(jnp.int32, (slots, planes * own), 1).astype(F32)
    low_half = lax.broadcasted_iota(jnp.int32, (width, 128), 1) < own
    held = jnp.concatenate([part[:cells] for part in parts], axis=1)
    flat = jnp.dot(turn, jnp.concatenate([held, held], axis=0), preferred_element_type=F32)
    ready = []
    for u, part in enumerate(parts):
        notes = part[cells:].astype(F32)
        keys = notes.T
        mine = flat[:, u * slots : (u + 1) * slots]
        for side in range(2):
            start = notes[3 * side : 3 * side + 1] * 32.0 + notes[3 * side + 1 : 3 * side + 2]
            cosine, sines = turn_cos_sin(wave_turns(wave * start.astype(jnp.int32), length))
            hot = jnp.where(place == keys[:, 3 * side + 2 : 3 * side + 3], 1.0, 0.0)
            turned = []
            for block in range(PD) if side == 0 else range(PD, 2 * PD - 1):
                real = mine[block * width : block * width + half]
                imag = mine[block * width + half : (block + 1) * width]
                turned.append((real * cosine + imag * sines).astype(BF16))
                turned.append((imag * cosine - real * sines).astype(BF16))
            ready.append((jnp.concatenate(turned, axis=0), hot.astype(BF16)))
    landed = [jnp.dot(left, hot, preferred_element_type=F32) for left, hot in ready]
    kept = []
    for u in range(len(parts)):
        mine = [landed[2 * u][a * width : (a + 1) * width] for a in range(PD)]
        below = [None] + [landed[2 * u + 1][a * width : (a + 1) * width] for a in range(PD - 1)]
        one = [mine[1][:, :128], jnp.where(low_half, mine[1][:, 128:], below[1][:, 128:])]
        two = [mine[2][:, :128], below[2][:, 128:]]
        three = [jnp.where(low_half, mine[3][:, :128], below[3][:, :128]), below[3][:, 128:]]
        odd = [pltpu.roll(one[0] + three[1], own, 1), pltpu.roll(one[1] + three[0], own, 1)]
        near = mine[0][:, :128] + two[1] + jnp.where(low_half, odd[1], odd[0])
        far = mine[0][:, 128:] + two[0] + jnp.where(low_half, odd[0], odd[1])
        kept.append(jnp.concatenate([near.T, far.T], axis=0).astype(BF16))
    return kept


def back_body(
    length, unroll, tiles,
    scal, spread, turn, lanes_of, table, spec, out,
    merged, basis, table_in, spec_in, out_from, sems, out_sems,
):
    planes, rows, width = spec_in.shape
    sources = spread.shape[0]
    own = rows // sources
    tile = rows // tiles
    loads = [
        pltpu.make_async_copy(table, table_in, sems.at[0]),
        pltpu.make_async_copy(spec, spec_in, sems.at[1]),
    ]
    for load in loads:
        load.start()

    def body(i, carry):
        parts = [spread[i * unroll + u] for u in range(unroll)]
        kept = merge_sources(length, scal[0], parts, turn[...], own, planes, width)
        for u in range(unroll):
            base = pl.multiple_of((i * unroll + u) * own, own)
            for x in range(planes):
                merged[x, pl.ds(base, own), :] = kept[u][x * own : (x + 1) * own]
        return carry

    lax.fori_loop(0, sources // unroll, body, 0)
    for x in range(planes):
        spaced = jnp.dot(merged[x], lanes_of[...], preferred_element_type=F32).astype(BF16)
        into = pl.ds(x * width, width)
        basis[pl.ds(0, rows), into] = spaced[:, :width]
        basis[pl.ds(rows, rows), into] = spaced[:, width:]
    for load in loads:
        load.wait()
    stores = []
    for t in range(tiles):
        span = pl.ds(t * tile, tile)
        mixed = jnp.dot(table_in[span, :], basis[...], preferred_element_type=F32)
        across = t * tile + lax.broadcasted_iota(jnp.int32, (tile, width), 0)
        along = scal[0] + lax.broadcasted_iota(jnp.int32, (tile, width), 1) // 2
        across_norm = jnp.minimum(across, rows - across).astype(F32) * (2.0 / rows)
        along_norm = jnp.minimum(along, length - along).astype(F32) * (2.0 / length)
        factor = 1.0 / (1.0 + across_norm * across_norm + along_norm * along_norm)
        for x in range(planes):
            cosine, sines = plane_phase(scal[1 + x], scal[0], width, length)
            values = spec_in[x, span, :]
            phased = values * cosine + rotate(values) * sines
            out_from[x, span, :] = factor * (phased + mixed[:, x * width : (x + 1) * width])
        store = pltpu.make_async_copy(out_from.at[:, span, :], out.at[:, span, :], out_sems.at[t])
        store.start()
        stores.append(store)
    for store in stores:
        store.wait()


def back_rows(scal, spread, turn, table, spec, length, unroll=8, tiles=4):
    planes, rows, width = spec.shape
    lanes_of = jnp.asarray(lane_table(width))
    whole = pl.BlockSpec(memory_space=pltpu.VMEM)
    away = pl.BlockSpec(memory_space=pl.ANY)
    return pl.pallas_call(
        functools.partial(back_body, length, unroll, tiles),
        in_specs=[pl.BlockSpec(memory_space=pltpu.SMEM), whole, whole, whole, away, away],
        out_specs=away,
        out_shape=jax.ShapeDtypeStruct((planes, rows, width), F32),
        scratch_shapes=[
            pltpu.VMEM((planes, rows, width), BF16),
            pltpu.VMEM((2 * rows, planes * width), BF16),
            pltpu.VMEM(table.shape, BF16),
            pltpu.VMEM(spec.shape, F32),
            pltpu.VMEM(spec.shape, F32),
            pltpu.SemaphoreType.DMA((2,)),
            pltpu.SemaphoreType.DMA((tiles,)),
        ],
        compiler_params=pltpu.CompilerParams(vmem_limit_bytes=VMEM_MIB * MIB),
        name="back_rows",
    )(scal, spread, turn, lanes_of, table, spec)


def one_slab_on(value, by):
    size = lax.axis_size("slab")
    return lax.ppermute(value, "slab", [(i, i + by) for i in range(size) if 0 <= i + by < size])


def shards(spec_vel, shear_shift, patch_pos, patch_count, interp_w, marker_vel):
    planes, rows, width = spec_vel.shape
    pencils = lax.axis_size("pencil")
    own = rows // pencils
    length = width // 2 * pencils
    slots = patch_pos.shape[-1]
    first_wave = (lax.axis_index("pencil") * (width // 2)).astype(jnp.int32)
    scal = jnp.concatenate([first_wave[None], shear_shift])
    table = jnp.asarray(row_table(rows))

    positions = patch_pos[0, 0]
    behind = one_slab_on(positions, 1)
    coefs = forward_rows(scal, spec_vel, table, own, length)
    coefs = coefs.reshape(pencils, planes * own, width)
    here = lax.all_to_all(coefs, "pencil", split_axis=0, concat_axis=0, tiled=True)
    notes = []
    for held in (positions, behind):
        notes += [held[2] // 32, held[2] % 32, held[0] * own + held[1]]
    notes = jnp.stack(notes + [jnp.zeros_like(notes[0])] * 2).astype(BF16)
    turn = spread_table(first_wave, width, length)
    here, turn, notes = lax.optimization_barrier((here, turn, notes))

    spots = patch_spots(positions, behind, own)
    field, above = above_cells(spots, here, jnp.asarray(depth_table(length)), slots)
    from_above = one_slab_on(above, -1)
    values = own_cells(spots, field, slots)
    forces, spread, upward = marker_forces(
        patch_count[0], interp_w[0, 0], values, from_above, marker_vel[0, 0]
    )
    from_below = one_slab_on(upward, 1)
    message = jnp.concatenate([spread, from_below, notes])[None]
    gathered = lax.all_gather(message, "pencil", axis=0, tiled=True)
    new_hat = back_rows(scal, gathered, turn, table, spec_vel, length)
    return (new_hat, forces[None, None])


def solution(mesh):
    placed = (
        P("slab", None, "pencil"),
        P("slab"),
        P("slab", "pencil", None, None),
        P("slab", "pencil"),
        P("slab", "pencil", None, None, None),
        P("slab", "pencil", None, None),
    )
    return jax.shard_map(
        shards,
        mesh=mesh,
        in_specs=placed,
        out_specs=(P("slab", None, "pencil"), P("slab", "pencil", None, None)),
        check_vma=False,
    )
```

```python
import functools
import math

import jax
import jax.numpy as jnp
import ml_dtypes
import numpy as np
from jax import lax
from jax.experimental import pallas as pl
from jax.experimental.pallas import tpu as pltpu
from jax.sharding import PartitionSpec as P

PD = 4
PZ = 16
MIB = 1 << 20
VMEM_MIB = 56
PITCH = 9
FIELD_TILES = 9
FIELD_PLANES = 15
F32 = jnp.float32
BF16 = jnp.bfloat16


def dft_tables(length):
    steps = np.arange(length, dtype=np.int64)
    turns = steps[:, None] * steps[None, :] % length
    angles = turns.astype(np.float32) * np.float32(2.0 * math.pi / length)
    norming = np.float32(1.0 / math.sqrt(length))
    return np.cos(angles) * norming, np.sin(angles) * norming


@functools.cache
def row_table(length):
    cosine, sines = dft_tables(length)
    return np.concatenate([cosine, sines], axis=1).astype(ml_dtypes.bfloat16)


@functools.cache
def depth_table(length):
    cosine, sines = dft_tables(length)
    merged = np.stack([cosine, -sines], axis=1).reshape(2 * length, length)
    return merged.astype(ml_dtypes.bfloat16)


def turn_cos_sin(turns):
    x = turns * math.pi
    x2 = x * x
    s = x * (
        1.0
        + x2
        * (
            -1.0 / 6
            + x2
            * (1.0 / 120 + x2 * (-1.0 / 5040 + x2 * (1.0 / 362880 + x2 * (-1.0 / 39916800))))
        )
    )
    c = 1.0 + x2 * (
        -0.5
        + x2
        * (1.0 / 24 + x2 * (-1.0 / 720 + x2 * (1.0 / 40320 + x2 * (-1.0 / 3628800))))
    )
    return 1.0 - 2.0 * s * s, 2.0 * s * c


def wave_turns(product, length):
    half = length // 2
    return (((product + half) & (length - 1)) - half).astype(F32) * (1.0 / length)


def rotate(values):
    width = values.shape[-1]
    lane = lax.broadcasted_iota(jnp.int32, values.shape, values.ndim - 1)
    axis = values.ndim - 1
    ahead = pltpu.roll(values, width - 1, axis)
    behind = pltpu.roll(values, 1, axis)
    return jnp.where(lane % 2 == 0, -ahead, behind)


def plane_phase(shift, first_wave, width, length):
    lane = lax.broadcasted_iota(jnp.int32, (1, width), 1)
    return turn_cos_sin(wave_turns((first_wave + lane // 2) * shift, length))


def forward_body(
    length, tiles, first, shifts, spec, table, out,
    basis, spec_in, table_in, out_from, sems, table_sems, out_sems,
):
    planes, rows, width = spec_in.shape
    dests, _, own, _ = out_from.shape
    tile = rows // tiles
    loads = [pltpu.make_async_copy(spec.at[x], spec_in.at[x], sems.at[x]) for x in range(planes)]
    spans = [pl.ds(t * tile, tile) for t in range(tiles)]
    tables = [
        pltpu.make_async_copy(table.at[span, :], table_in.at[span, :], table_sems.at[t])
        for t, span in enumerate(spans)
    ]
    for load in loads + tables:
        load.start()
    for x in range(planes):
        loads[x].wait()
        cosine, sines = plane_phase(shifts[x], first[0], width, length)
        values = spec_in[x]
        turned = rotate(values)
        lanes = pl.ds(x * width, width)
        basis[pl.ds(0, rows), lanes] = (values * cosine + turned * sines).astype(BF16)
        basis[pl.ds(rows, rows), lanes] = (turned * cosine - values * sines).astype(BF16)
    stores = []
    group = dests // tiles
    for t, span in enumerate(spans):
        tables[t].wait()
        mixed = jnp.dot(table_in[span, :], basis[...], preferred_element_type=F32).astype(BF16)
        for d in range(group):
            for x in range(planes):
                out_from[t * group + d, x] = mixed[
                    d * own : (d + 1) * own, x * width : (x + 1) * width
                ]
        ready = pl.ds(t * group, group)
        store = pltpu.make_async_copy(out_from.at[ready], out.at[ready], out_sems.at[t])
        store.start()
        stores.append(store)
    for store in stores:
        store.wait()


def forward_rows(first, shifts, spec, table, own, length, tiles=2):
    planes, rows, width = spec.shape
    small = pl.BlockSpec(memory_space=pltpu.SMEM)
    away = pl.BlockSpec(memory_space=pl.ANY)
    shape = (rows // own, planes, own, width)
    return pl.pallas_call(
        functools.partial(forward_body, length, tiles),
        in_specs=[small, small, away, away],
        out_specs=away,
        out_shape=jax.ShapeDtypeStruct(shape, BF16),
        scratch_shapes=[
            pltpu.VMEM((2 * rows, planes * width), BF16),
            pltpu.VMEM(spec.shape, F32),
            pltpu.VMEM(table.shape, BF16),
            pltpu.VMEM(shape, BF16),
            pltpu.SemaphoreType.DMA((planes,)),
            pltpu.SemaphoreType.DMA((tiles,)),
            pltpu.SemaphoreType.DMA((tiles,)),
        ],
        compiler_params=pltpu.CompilerParams(vmem_limit_bytes=VMEM_MIB * MIB),
        name="forward_rows",
    )(first, shifts, spec, table)


def fetch_body(source, out, sem):
    copy = pltpu.make_async_copy(source, out, sem)
    copy.start()
    copy.wait()


def fetched(table):
    return pl.pallas_call(
        fetch_body,
        in_specs=[pl.BlockSpec(memory_space=pl.ANY)],
        out_specs=pl.BlockSpec(memory_space=pltpu.VMEM),
        out_shape=jax.ShapeDtypeStruct(table.shape, table.dtype),
        scratch_shapes=[pltpu.SemaphoreType.DMA],
        compiler_params=pltpu.CompilerParams(vmem_limit_bytes=16 * MIB),
        name="fetch_table",
    )(table)


def take_cells(spots, field, into, base, slots):
    lane = lax.broadcasted_iota(jnp.int32, (8, 128), 1)
    pitch = field.shape[0] // FIELD_TILES
    span = pitch // FIELD_PLANES
    batch = 16

    def body(i, carry):
        found = []
        for u in range(batch):
            spot = spots[base + i * batch + u]
            off = spots[base + slots + i * batch + u]
            near = field[pl.ds(spot, 8, stride=span), :]
            far = field[pl.ds(spot + pitch, 8, stride=span), :]
            found.append(pltpu.roll(jnp.where(lane >= off, near, far), 128 - off, 1))
        for u in range(batch):
            into[pl.ds((i * batch + u) * PITCH, 8), :] = found[u]
        return carry

    lax.fori_loop(0, slots // batch, body, 0)


def cells_first(into, slots):
    wide = lax.broadcasted_iota(jnp.int32, (slots, 128), 1) < PZ
    total = jnp.where(wide, into[pl.ds(0, slots, stride=PITCH), :], 0.0)
    for a in range(1, PD):
        part = jnp.where(wide, into[pl.ds(a, slots, stride=PITCH), :], 0.0)
        total += pltpu.roll(part, a * PZ, 1)
    return total.T


def above_body(slots, tiles, spots, coefs, table, field, above_out, into):
    sources, rows, width = coefs.shape
    own = rows // PD
    span = own + 1
    pitch = FIELD_PLANES * span
    blank = jnp.zeros((PD * span, 128), F32)
    for t in range(FIELD_TILES):
        field[pl.ds(t * pitch, PD * span), :] = blank
        field[pl.ds(t * pitch + 2 * PD * span, (PD - 1) * span), :] = blank[span:]
    field[pl.ds((FIELD_TILES - 1) * pitch + PD * span, PD * span), :] = blank
    left = jnp.concatenate([coefs[j] for j in range(sources)], axis=1)
    size = table.shape[1] // tiles
    parts = size // 128
    for t in range(tiles):
        velocity = jnp.dot(
            left, table[:, t * size : (t + 1) * size], preferred_element_type=F32
        )
        for j in range(parts):
            for x in range(PD):
                start = (parts * t + j) * pitch + (PD + x) * span
                field[pl.ds(start, own), :] = velocity[
                    x * own : (x + 1) * own, j * 128 : (j + 1) * 128
                ]
    take_cells(spots, field, into, 2 * slots, slots)
    above_out[...] = cells_first(into, slots)[PZ : PD * PZ]


def patch_spots(positions, behind, own):
    parts = []
    for held, lift in ((positions, PD), (behind, 0)):
        tile = held[2] // 128
        parts.append(
            (tile * FIELD_PLANES + held[0] + lift) * (own + 1) + held[1]
        )
        parts.append(held[2] % 128)
    return jnp.concatenate(parts)


def own_body(slots, pos, field, own_out, into):
    take_cells(pos, field, into, 0, slots)
    own_out[...] = cells_first(into, slots)[: PD * PZ]


def above_cells(spots, coefs, table, slots, tiles=2):
    rows = coefs.shape[1]
    span = rows // PD + 1
    field_shape = (FIELD_TILES * FIELD_PLANES * span, 128)
    whole = pl.BlockSpec(memory_space=pltpu.VMEM)
    return pl.pallas_call(
        functools.partial(above_body, slots, tiles),
        in_specs=[pl.BlockSpec(memory_space=pltpu.SMEM), whole, whole],
        out_specs=[whole, whole],
        out_shape=[
            jax.ShapeDtypeStruct(field_shape, F32),
            jax.ShapeDtypeStruct(((PD - 1) * PZ, slots), F32),
        ],
        scratch_shapes=[pltpu.VMEM((slots * PITCH, 128), F32)],
        compiler_params=pltpu.CompilerParams(vmem_limit_bytes=24 * MIB),
        name="above_cells",
    )(spots, coefs, table)


def own_cells(pos, field, slots):
    return pl.pallas_call(
        functools.partial(own_body, slots),
        in_specs=[
            pl.BlockSpec(memory_space=pltpu.SMEM),
            pl.BlockSpec(memory_space=pltpu.VMEM),
        ],
        out_specs=pl.BlockSpec(memory_space=pltpu.VMEM),
        out_shape=jax.ShapeDtypeStruct((PD * PZ, slots), F32),
        scratch_shapes=[pltpu.VMEM((slots * PITCH, 128), F32)],
        compiler_params=pltpu.CompilerParams(vmem_limit_bytes=24 * MIB),
        name="own_cells",
    )(pos, field)


def force_body(count, weights, own, above, target, forces, own_out, up_out, values, spread):
    step = pl.program_id(0)
    markers, cells, slots = weights.shape

    @pl.when(step == 0)
    def _():
        values[pl.ds(0, PZ), :] = own[pl.ds(0, PZ), :]
        values[pl.ds(PZ, cells - PZ), :] = own[pl.ds(PZ, cells - PZ), :] + above[...]
        spread[...] = jnp.zeros((cells, slots), F32)

    live = lax.broadcasted_iota(jnp.int32, (1, slots), 1) < count[0]
    held = values[...]
    total = spread[...]
    for m in range(markers):
        wide = weights[m].astype(F32)
        interp = jnp.sum(wide * held, axis=0, keepdims=True)
        force = jnp.where(live, target[pl.ds(m, 1), :] - interp, 0.0)
        forces[pl.ds(m, 1), :] = force
        total = total + wide * force
    spread[...] = total

    @pl.when(step == pl.num_programs(0) - 1)
    def _():
        own_out[...] = total.astype(BF16)
        up_out[...] = total[PZ:].astype(BF16)


def marker_forces(count, weights, own, above, target):
    markers, cells, slots = weights.shape
    steps = 4
    tile = markers // steps
    whole = lambda i: (0, 0)
    return pl.pallas_call(
        force_body,
        grid=(steps,),
        in_specs=[
            pl.BlockSpec(memory_space=pltpu.SMEM),
            pl.BlockSpec((tile, cells, slots), lambda i: (i, 0, 0)),
            pl.BlockSpec((cells, slots), whole),
            pl.BlockSpec((cells - PZ, slots), whole),
            pl.BlockSpec((tile, slots), lambda i: (i, 0)),
        ],
        out_specs=[
            pl.BlockSpec((tile, slots), lambda i: (i, 0)),
            pl.BlockSpec((cells, slots), whole),
            pl.BlockSpec((cells - PZ, slots), whole),
        ],
        out_shape=[
            jax.ShapeDtypeStruct((markers, slots), F32),
            jax.ShapeDtypeStruct((cells, slots), BF16),
            jax.ShapeDtypeStruct((cells - PZ, slots), BF16),
        ],
        scratch_shapes=[pltpu.VMEM((cells, slots), F32), pltpu.VMEM((cells, slots), F32)],
        compiler_params=pltpu.CompilerParams(vmem_limit_bytes=32 * MIB),
        name="marker_forces",
    )(count, weights, own, above, target)


def spread_table(first_wave, width, length):
    half = width // 2
    row = jnp.arange(width, dtype=jnp.int32)[:, None]
    cell = jnp.arange(PZ, dtype=jnp.int32)[None, :]
    wave = first_wave + row % half
    cosine, sines = turn_cos_sin(wave_turns(wave * cell, length))
    entry = jnp.where(row < half, cosine, -sines) * (1.0 / math.sqrt(length))
    high = entry.astype(BF16)
    low = (entry - high.astype(F32)).astype(BF16)
    blocks = 2 * PD - 1
    eye = jnp.eye(blocks, dtype=BF16)
    halves = [
        (eye[:, None, :, None] * part[None, :, None, :]).reshape(blocks * width, blocks * PZ)
        for part in (high, low)
    ]
    return jnp.concatenate(halves, axis=1)


def lane_table(width):
    half = width // 2
    table = np.zeros((width, 2 * width), np.float32)
    for k in range(half):
        table[k, 2 * k] = 1.0
        table[half + k, 2 * k + 1] = 1.0
        table[half + k, width + 2 * k] = 1.0
        table[k, width + 2 * k + 1] = -1.0
    return table.astype(ml_dtypes.bfloat16)


def merge_sources(length, first_wave, parts, turn, own, planes, width):
    half = width // 2
    cells = (2 * PD - 1) * PZ
    slots = parts[0].shape[1]
    wave = first_wave + lax.broadcasted_iota(jnp.int32, (half, 1), 0)
    place = lax.broadcasted_iota(jnp.int32, (slots, planes * own), 1).astype(F32)
    low_half = lax.broadcasted_iota(jnp.int32, (width, 128), 1) < own
    held = jnp.concatenate([part[:cells] for part in parts], axis=1)
    flat = jnp.dot(turn, jnp.concatenate([held, held], axis=0), preferred_element_type=F32)
    ready = []
    for u, part in enumerate(parts):
        notes = part[cells:].astype(F32)
        keys = notes.T
        mine = flat[:, u * slots : (u + 1) * slots]
        for side in range(2):
            start = notes[3 * side : 3 * side + 1] * 32.0 + notes[3 * side + 1 : 3 * side + 2]
            cosine, sines = turn_cos_sin(wave_turns(wave * start.astype(jnp.int32), length))
            hot = jnp.where(place == keys[:, 3 * side + 2 : 3 * side + 3], 1.0, 0.0)
            turned = []
            for block in range(PD) if side == 0 else range(PD, 2 * PD - 1):
                real = mine[block * width : block * width + half]
                imag = mine[block * width + half : (block + 1) * width]
                turned.append((real * cosine + imag * sines).astype(BF16))
                turned.append((imag * cosine - real * sines).astype(BF16))
            ready.append((jnp.concatenate(turned, axis=0), hot.astype(BF16)))
    landed = [jnp.dot(left, hot, preferred_element_type=F32) for left, hot in ready]
    kept = []
    for u in range(len(parts)):
        mine = [landed[2 * u][a * width : (a + 1) * width] for a in range(PD)]
        below = [None] + [landed[2 * u + 1][a * width : (a + 1) * width] for a in range(PD - 1)]
        one = [mine[1][:, :128], jnp.where(low_half, mine[1][:, 128:], below[1][:, 128:])]
        two = [mine[2][:, :128], below[2][:, 128:]]
        three = [jnp.where(low_half, mine[3][:, :128], below[3][:, :128]), below[3][:, 128:]]
        odd = [pltpu.roll(one[0] + three[1], own, 1), pltpu.roll(one[1] + three[0], own, 1)]
        near = mine[0][:, :128] + two[1] + jnp.where(low_half, odd[1], odd[0])
        far = mine[0][:, 128:] + two[0] + jnp.where(low_half, odd[0], odd[1])
        kept.append(jnp.concatenate([near.T, far.T], axis=0).astype(BF16))
    return kept


def back_body(
    length, unroll, tiles,
    first, shifts, spread, turn, lanes_of, table, spec, out,
    merged, basis, table_in, spec_in, out_from, sems, out_sems,
):
    planes, rows, width = spec_in.shape
    sources = spread.shape[0]
    own = rows // sources
    tile = rows // tiles
    loads = [
        pltpu.make_async_copy(table, table_in, sems.at[0]),
        pltpu.make_async_copy(spec, spec_in, sems.at[1]),
    ]
    for load in loads:
        load.start()

    def body(i, carry):
        parts = [spread[i * unroll + u] for u in range(unroll)]
        kept = merge_sources(length, first[0], parts, turn[...], own, planes, width)
        for u in range(unroll):
            base = pl.multiple_of((i * unroll + u) * own, own)
            for x in range(planes):
                merged[x, pl.ds(base, own), :] = kept[u][x * own : (x + 1) * own]
        return carry

    lax.fori_loop(0, sources // unroll, body, 0)
    for x in range(planes):
        spaced = jnp.dot(merged[x], lanes_of[...], preferred_element_type=F32).astype(BF16)
        into = pl.ds(x * width, width)
        basis[pl.ds(0, rows), into] = spaced[:, :width]
        basis[pl.ds(rows, rows), into] = spaced[:, width:]
    for load in loads:
        load.wait()
    stores = []
    for t in range(tiles):
        span = pl.ds(t * tile, tile)
        mixed = jnp.dot(table_in[span, :], basis[...], preferred_element_type=F32)
        across = t * tile + lax.broadcasted_iota(jnp.int32, (tile, width), 0)
        along = first[0] + lax.broadcasted_iota(jnp.int32, (tile, width), 1) // 2
        across_norm = jnp.minimum(across, rows - across).astype(F32) * (2.0 / rows)
        along_norm = jnp.minimum(along, length - along).astype(F32) * (2.0 / length)
        factor = 1.0 / (1.0 + across_norm * across_norm + along_norm * along_norm)
        for x in range(planes):
            cosine, sines = plane_phase(shifts[x], first[0], width, length)
            values = spec_in[x, span, :]
            phased = values * cosine + rotate(values) * sines
            out_from[x, span, :] = factor * (phased + mixed[:, x * width : (x + 1) * width])
        store = pltpu.make_async_copy(out_from.at[:, span, :], out.at[:, span, :], out_sems.at[t])
        store.start()
        stores.append(store)
    for store in stores:
        store.wait()


def back_rows(first, shifts, spread, turn, table, spec, length, unroll=8, tiles=4):
    planes, rows, width = spec.shape
    lanes_of = jnp.asarray(lane_table(width))
    small = pl.BlockSpec(memory_space=pltpu.SMEM)
    whole = pl.BlockSpec(memory_space=pltpu.VMEM)
    away = pl.BlockSpec(memory_space=pl.ANY)
    return pl.pallas_call(
        functools.partial(back_body, length, unroll, tiles),
        in_specs=[small, small, whole, whole, whole, away, away],
        out_specs=away,
        out_shape=jax.ShapeDtypeStruct((planes, rows, width), F32),
        scratch_shapes=[
            pltpu.VMEM((planes, rows, width), BF16),
            pltpu.VMEM((2 * rows, planes * width), BF16),
            pltpu.VMEM(table.shape, BF16),
            pltpu.VMEM(spec.shape, F32),
            pltpu.VMEM(spec.shape, F32),
            pltpu.SemaphoreType.DMA((2,)),
            pltpu.SemaphoreType.DMA((tiles,)),
        ],
        compiler_params=pltpu.CompilerParams(vmem_limit_bytes=VMEM_MIB * MIB),
        name="back_rows",
    )(first, shifts, spread, turn, lanes_of, table, spec)


def one_slab_on(value, by):
    size = lax.axis_size("slab")
    return lax.ppermute(value, "slab", [(i, i + by) for i in range(size) if 0 <= i + by < size])


def shards(spec_vel, shear_shift, patch_pos, patch_count, interp_w, marker_vel):
    planes, rows, width = spec_vel.shape
    pencils = lax.axis_size("pencil")
    own = rows // pencils
    length = width // 2 * pencils
    slots = patch_pos.shape[-1]
    first_wave = (lax.axis_index("pencil") * (width // 2)).astype(jnp.int32)
    first = first_wave[None]
    table = jnp.asarray(row_table(rows))

    positions = patch_pos[0, 0]
    coefs = forward_rows(first, shear_shift, spec_vel, table, own, length)
    positions, wave_table, coefs = lax.optimization_barrier(
        (positions, jnp.asarray(depth_table(length)), coefs)
    )
    behind = one_slab_on(positions, 1)
    wave_table = fetched(wave_table)
    coefs = coefs.reshape(pencils, planes * own, width)
    here = lax.all_to_all(coefs, "pencil", split_axis=0, concat_axis=0, tiled=True)
    notes = []
    for held in (positions, behind):
        notes += [held[2] // 32, held[2] % 32, held[0] * own + held[1]]
    notes = jnp.stack(notes + [jnp.zeros_like(notes[0])] * 2).astype(BF16)
    turn = spread_table(first_wave, width, length)
    here, turn, notes, wave_table = lax.optimization_barrier((here, turn, notes, wave_table))

    spots = patch_spots(positions, behind, own)
    field, above = above_cells(spots, here, wave_table, slots)
    from_above = one_slab_on(above, -1)
    values = own_cells(spots, field, slots)
    forces, spread, upward = marker_forces(
        patch_count[0], interp_w[0, 0], values, from_above, marker_vel[0, 0]
    )
    from_below = one_slab_on(upward, 1)
    message = jnp.concatenate([spread, from_below, notes])[None]
    gathered = lax.all_gather(message, "pencil", axis=0, tiled=True)
    new_hat = back_rows(first, shear_shift, gathered, turn, table, spec_vel, length)
    return (new_hat, forces[None, None])


def solution(mesh):
    placed = (
        P("slab", None, "pencil"),
        P("slab"),
        P("slab", "pencil", None, None),
        P("slab", "pencil"),
        P("slab", "pencil", None, None, None),
        P("slab", "pencil", None, None),
    )
    return jax.shard_map(
        shards,
        mesh=mesh,
        in_specs=placed,
        out_specs=(P("slab", None, "pencil"), P("slab", "pencil", None, None)),
        check_vma=False,
    )
```

```python
import functools
import math

import jax
import jax.numpy as jnp
import ml_dtypes
import numpy as np
from jax import lax
from jax.experimental import pallas as pl
from jax.experimental.pallas import tpu as pltpu
from jax.sharding import PartitionSpec as P

PD = 4
PZ = 16
MIB = 1 << 20
VMEM_MIB = 56
PITCH = 9
FIELD_TILES = 9
FIELD_PLANES = 15
F32 = jnp.float32
BF16 = jnp.bfloat16


def dft_tables(length):
    steps = np.arange(length, dtype=np.int64)
    turns = steps[:, None] * steps[None, :] % length
    angles = turns.astype(np.float32) * np.float32(2.0 * math.pi / length)
    norming = np.float32(1.0 / math.sqrt(length))
    return np.cos(angles) * norming, np.sin(angles) * norming


@functools.cache
def row_table(length):
    cosine, sines = dft_tables(length)
    return np.concatenate([cosine, sines], axis=1).astype(ml_dtypes.bfloat16)


@functools.cache
def depth_table(length):
    cosine, sines = dft_tables(length)
    merged = np.stack([cosine, -sines], axis=1).reshape(2 * length, length)
    return merged.astype(ml_dtypes.bfloat16)


def turn_cos_sin(turns):
    x = turns * math.pi
    x2 = x * x
    s = x * (
        1.0
        + x2
        * (
            -1.0 / 6
            + x2
            * (1.0 / 120 + x2 * (-1.0 / 5040 + x2 * (1.0 / 362880 + x2 * (-1.0 / 39916800))))
        )
    )
    c = 1.0 + x2 * (
        -0.5
        + x2
        * (1.0 / 24 + x2 * (-1.0 / 720 + x2 * (1.0 / 40320 + x2 * (-1.0 / 3628800))))
    )
    return 1.0 - 2.0 * s * s, 2.0 * s * c


def wave_turns(product, length):
    half = length // 2
    return (((product + half) & (length - 1)) - half).astype(F32) * (1.0 / length)


def rotate(values):
    width = values.shape[-1]
    lane = lax.broadcasted_iota(jnp.int32, values.shape, values.ndim - 1)
    axis = values.ndim - 1
    ahead = pltpu.roll(values, width - 1, axis)
    behind = pltpu.roll(values, 1, axis)
    return jnp.where(lane % 2 == 0, -ahead, behind)


def plane_phase(shift, first_wave, width, length):
    lane = lax.broadcasted_iota(jnp.int32, (1, width), 1)
    return turn_cos_sin(wave_turns((first_wave + lane // 2) * shift, length))


def forward_body(
    length, tiles, first, shifts, spec, table, out,
    basis, spec_in, table_in, out_from, sems, table_sems, out_sems,
):
    planes, rows, width = spec_in.shape
    dests, _, own, _ = out_from.shape
    tile = rows // tiles
    loads = [pltpu.make_async_copy(spec.at[x], spec_in.at[x], sems.at[x]) for x in range(planes)]
    spans = [pl.ds(t * tile, tile) for t in range(tiles)]
    tables = [
        pltpu.make_async_copy(table.at[span, :], table_in.at[span, :], table_sems.at[t])
        for t, span in enumerate(spans)
    ]
    for load in loads + tables:
        load.start()
    for x in range(planes):
        loads[x].wait()
        cosine, sines = plane_phase(shifts[x], first[0], width, length)
        values = spec_in[x]
        turned = rotate(values)
        lanes = pl.ds(x * width, width)
        basis[pl.ds(0, rows), lanes] = (values * cosine + turned * sines).astype(BF16)
        basis[pl.ds(rows, rows), lanes] = (turned * cosine - values * sines).astype(BF16)
    stores = []
    group = dests // tiles
    for t, span in enumerate(spans):
        tables[t].wait()
        mixed = jnp.dot(table_in[span, :], basis[...], preferred_element_type=F32).astype(BF16)
        for d in range(group):
            for x in range(planes):
                out_from[t * group + d, x] = mixed[
                    d * own : (d + 1) * own, x * width : (x + 1) * width
                ]
        ready = pl.ds(t * group, group)
        store = pltpu.make_async_copy(out_from.at[ready], out.at[ready], out_sems.at[t])
        store.start()
        stores.append(store)
    for store in stores:
        store.wait()


def forward_rows(first, shifts, spec, table, own, length, tiles=2):
    planes, rows, width = spec.shape
    small = pl.BlockSpec(memory_space=pltpu.SMEM)
    away = pl.BlockSpec(memory_space=pl.ANY)
    shape = (rows // own, planes, own, width)
    return pl.pallas_call(
        functools.partial(forward_body, length, tiles),
        in_specs=[small, small, away, away],
        out_specs=away,
        out_shape=jax.ShapeDtypeStruct(shape, BF16),
        scratch_shapes=[
            pltpu.VMEM((2 * rows, planes * width), BF16),
            pltpu.VMEM(spec.shape, F32),
            pltpu.VMEM(table.shape, BF16),
            pltpu.VMEM(shape, BF16),
            pltpu.SemaphoreType.DMA((planes,)),
            pltpu.SemaphoreType.DMA((tiles,)),
            pltpu.SemaphoreType.DMA((tiles,)),
        ],
        compiler_params=pltpu.CompilerParams(vmem_limit_bytes=VMEM_MIB * MIB),
        name="forward_rows",
    )(first, shifts, spec, table)


def take_cells(spots, field, into, base, slots):
    lane = lax.broadcasted_iota(jnp.int32, (8, 128), 1)
    pitch = field.shape[0] // FIELD_TILES
    span = pitch // FIELD_PLANES
    batch = 16

    def body(i, carry):
        found = []
        for u in range(batch):
            spot = spots[base + i * batch + u]
            off = spots[base + slots + i * batch + u]
            near = field[pl.ds(spot, 8, stride=span), :]
            far = field[pl.ds(spot + pitch, 8, stride=span), :]
            found.append(pltpu.roll(jnp.where(lane >= off, near, far), 128 - off, 1))
        for u in range(batch):
            into[pl.ds((i * batch + u) * PITCH, 8), :] = found[u]
        return carry

    lax.fori_loop(0, slots // batch, body, 0)


def cells_first(into, slots):
    wide = lax.broadcasted_iota(jnp.int32, (slots, 128), 1) < PZ
    total = jnp.where(wide, into[pl.ds(0, slots, stride=PITCH), :], 0.0)
    for a in range(1, PD):
        part = jnp.where(wide, into[pl.ds(a, slots, stride=PITCH), :], 0.0)
        total += pltpu.roll(part, a * PZ, 1)
    return total.T


def above_body(slots, tiles, spots, coefs, table, field, above_out, into):
    sources, rows, width = coefs.shape
    own = rows // PD
    span = own + 1
    pitch = FIELD_PLANES * span
    blank = jnp.zeros((PD * span, 128), F32)
    for t in range(FIELD_TILES):
        field[pl.ds(t * pitch, PD * span), :] = blank
        field[pl.ds(t * pitch + 2 * PD * span, (PD - 1) * span), :] = blank[span:]
    field[pl.ds((FIELD_TILES - 1) * pitch + PD * span, PD * span), :] = blank
    left = jnp.concatenate([coefs[j] for j in range(sources)], axis=1)
    size = table.shape[1] // tiles
    parts = size // 128
    for t in range(tiles):
        velocity = jnp.dot(
            left, table[:, t * size : (t + 1) * size], preferred_element_type=F32
        )
        for j in range(parts):
            for x in range(PD):
                start = (parts * t + j) * pitch + (PD + x) * span
                field[pl.ds(start, own), :] = velocity[
                    x * own : (x + 1) * own, j * 128 : (j + 1) * 128
                ]
    take_cells(spots, field, into, 2 * slots, slots)
    above_out[...] = cells_first(into, slots)[PZ : PD * PZ]


def patch_spots(positions, behind, own):
    parts = []
    for held, lift in ((positions, PD), (behind, 0)):
        tile = held[2] // 128
        parts.append(
            (tile * FIELD_PLANES + held[0] + lift) * (own + 1) + held[1]
        )
        parts.append(held[2] % 128)
    return jnp.concatenate(parts)


def own_body(slots, pos, field, own_out, into):
    take_cells(pos, field, into, 0, slots)
    own_out[...] = cells_first(into, slots)[: PD * PZ]


def above_cells(spots, coefs, table, slots, tiles=2):
    rows = coefs.shape[1]
    span = rows // PD + 1
    field_shape = (FIELD_TILES * FIELD_PLANES * span, 128)
    whole = pl.BlockSpec(memory_space=pltpu.VMEM)
    return pl.pallas_call(
        functools.partial(above_body, slots, tiles),
        in_specs=[pl.BlockSpec(memory_space=pltpu.SMEM), whole, whole],
        out_specs=[whole, whole],
        out_shape=[
            jax.ShapeDtypeStruct(field_shape, F32),
            jax.ShapeDtypeStruct(((PD - 1) * PZ, slots), F32),
        ],
        scratch_shapes=[pltpu.VMEM((slots * PITCH, 128), F32)],
        compiler_params=pltpu.CompilerParams(vmem_limit_bytes=24 * MIB),
        name="above_cells",
    )(spots, coefs, table)


def own_cells(pos, field, slots):
    return pl.pallas_call(
        functools.partial(own_body, slots),
        in_specs=[
            pl.BlockSpec(memory_space=pltpu.SMEM),
            pl.BlockSpec(memory_space=pltpu.VMEM),
        ],
        out_specs=pl.BlockSpec(memory_space=pltpu.VMEM),
        out_shape=jax.ShapeDtypeStruct((PD * PZ, slots), F32),
        scratch_shapes=[pltpu.VMEM((slots * PITCH, 128), F32)],
        compiler_params=pltpu.CompilerParams(vmem_limit_bytes=24 * MIB),
        name="own_cells",
    )(pos, field)


def force_body(count, weights, own, above, target, forces, own_out, up_out, values, spread):
    step = pl.program_id(0)
    markers, cells, slots = weights.shape

    @pl.when(step == 0)
    def _():
        values[pl.ds(0, PZ), :] = own[pl.ds(0, PZ), :]
        values[pl.ds(PZ, cells - PZ), :] = own[pl.ds(PZ, cells - PZ), :] + above[...]
        spread[...] = jnp.zeros((cells, slots), F32)

    live = lax.broadcasted_iota(jnp.int32, (1, slots), 1) < count[0]
    held = values[...]
    total = spread[...]
    for m in range(markers):
        wide = weights[m].astype(F32)
        interp = jnp.sum(wide * held, axis=0, keepdims=True)
        force = jnp.where(live, target[pl.ds(m, 1), :] - interp, 0.0)
        forces[pl.ds(m, 1), :] = force
        total = total + wide * force
    spread[...] = total

    @pl.when(step == pl.num_programs(0) - 1)
    def _():
        own_out[...] = total.astype(BF16)
        up_out[...] = total[PZ:].astype(BF16)


def marker_forces(count, weights, own, above, target):
    markers, cells, slots = weights.shape
    steps = 4
    tile = markers // steps
    whole = lambda i: (0, 0)
    return pl.pallas_call(
        force_body,
        grid=(steps,),
        in_specs=[
            pl.BlockSpec(memory_space=pltpu.SMEM),
            pl.BlockSpec((tile, cells, slots), lambda i: (i, 0, 0)),
            pl.BlockSpec((cells, slots), whole),
            pl.BlockSpec((cells - PZ, slots), whole),
            pl.BlockSpec((tile, slots), lambda i: (i, 0)),
        ],
        out_specs=[
            pl.BlockSpec((tile, slots), lambda i: (i, 0)),
            pl.BlockSpec((cells, slots), whole),
            pl.BlockSpec((cells - PZ, slots), whole),
        ],
        out_shape=[
            jax.ShapeDtypeStruct((markers, slots), F32),
            jax.ShapeDtypeStruct((cells, slots), BF16),
            jax.ShapeDtypeStruct((cells - PZ, slots), BF16),
        ],
        scratch_shapes=[pltpu.VMEM((cells, slots), F32), pltpu.VMEM((cells, slots), F32)],
        compiler_params=pltpu.CompilerParams(vmem_limit_bytes=32 * MIB),
        name="marker_forces",
    )(count, weights, own, above, target)


def spread_table(first_wave, width, length):
    half = width // 2
    row = jnp.arange(width, dtype=jnp.int32)[:, None]
    cell = jnp.arange(PZ, dtype=jnp.int32)[None, :]
    wave = first_wave + row % half
    cosine, sines = turn_cos_sin(wave_turns(wave * cell, length))
    entry = jnp.where(row < half, cosine, -sines) * (1.0 / math.sqrt(length))
    high = entry.astype(BF16)
    low = (entry - high.astype(F32)).astype(BF16)
    blocks = 2 * PD - 1
    eye = jnp.eye(blocks, dtype=BF16)
    halves = [
        (eye[:, None, :, None] * part[None, :, None, :]).reshape(blocks * width, blocks * PZ)
        for part in (high, low)
    ]
    return jnp.concatenate(halves, axis=1)


def lane_table(width):
    half = width // 2
    table = np.zeros((width, 2 * width), np.float32)
    for k in range(half):
        table[k, 2 * k] = 1.0
        table[half + k, 2 * k + 1] = 1.0
        table[half + k, width + 2 * k] = 1.0
        table[k, width + 2 * k + 1] = -1.0
    return table.astype(ml_dtypes.bfloat16)


def merge_sources(length, first_wave, parts, turn, own, planes, width):
    half = width // 2
    cells = (2 * PD - 1) * PZ
    slots = parts[0].shape[1]
    wave = first_wave + lax.broadcasted_iota(jnp.int32, (half, 1), 0)
    place = lax.broadcasted_iota(jnp.int32, (slots, planes * own), 1).astype(F32)
    low_half = lax.broadcasted_iota(jnp.int32, (width, 128), 1) < own
    held = jnp.concatenate([part[:cells] for part in parts], axis=1)
    flat = jnp.dot(turn, jnp.concatenate([held, held], axis=0), preferred_element_type=F32)
    ready = []
    for u, part in enumerate(parts):
        notes = part[cells:].astype(F32)
        keys = notes.T
        mine = flat[:, u * slots : (u + 1) * slots]
        for side in range(2):
            start = notes[3 * side : 3 * side + 1] * 32.0 + notes[3 * side + 1 : 3 * side + 2]
            cosine, sines = turn_cos_sin(wave_turns(wave * start.astype(jnp.int32), length))
            hot = jnp.where(place == keys[:, 3 * side + 2 : 3 * side + 3], 1.0, 0.0)
            turned = []
            for block in range(PD) if side == 0 else range(PD, 2 * PD - 1):
                real = mine[block * width : block * width + half]
                imag = mine[block * width + half : (block + 1) * width]
                turned.append((real * cosine + imag * sines).astype(BF16))
                turned.append((imag * cosine - real * sines).astype(BF16))
            ready.append((jnp.concatenate(turned, axis=0), hot.astype(BF16)))
    landed = [jnp.dot(left, hot, preferred_element_type=F32) for left, hot in ready]
    kept = []
    for u in range(len(parts)):
        mine = [landed[2 * u][a * width : (a + 1) * width] for a in range(PD)]
        below = [None] + [landed[2 * u + 1][a * width : (a + 1) * width] for a in range(PD - 1)]
        one = [mine[1][:, :128], jnp.where(low_half, mine[1][:, 128:], below[1][:, 128:])]
        two = [mine[2][:, :128], below[2][:, 128:]]
        three = [jnp.where(low_half, mine[3][:, :128], below[3][:, :128]), below[3][:, 128:]]
        odd = [pltpu.roll(one[0] + three[1], own, 1), pltpu.roll(one[1] + three[0], own, 1)]
        near = mine[0][:, :128] + two[1] + jnp.where(low_half, odd[1], odd[0])
        far = mine[0][:, 128:] + two[0] + jnp.where(low_half, odd[0], odd[1])
        kept.append(jnp.concatenate([near.T, far.T], axis=0).astype(BF16))
    return kept


def back_body(
    length, unroll, tiles,
    first, shifts, spread, turn, lanes_of, table, spec, out,
    merged, basis, table_in, spec_in, out_from, sems, out_sems,
):
    planes, rows, width = spec_in.shape
    sources = spread.shape[0]
    own = rows // sources
    tile = rows // tiles
    loads = [
        pltpu.make_async_copy(table, table_in, sems.at[0]),
        pltpu.make_async_copy(spec, spec_in, sems.at[1]),
    ]
    for load in loads:
        load.start()

    def body(i, carry):
        parts = [spread[i * unroll + u] for u in range(unroll)]
        kept = merge_sources(length, first[0], parts, turn[...], own, planes, width)
        for u in range(unroll):
            base = pl.multiple_of((i * unroll + u) * own, own)
            for x in range(planes):
                merged[x, pl.ds(base, own), :] = kept[u][x * own : (x + 1) * own]
        return carry

    lax.fori_loop(0, sources // unroll, body, 0)
    for x in range(planes):
        spaced = jnp.dot(merged[x], lanes_of[...], preferred_element_type=F32).astype(BF16)
        into = pl.ds(x * width, width)
        basis[pl.ds(0, rows), into] = spaced[:, :width]
        basis[pl.ds(rows, rows), into] = spaced[:, width:]
    for load in loads:
        load.wait()
    stores = []
    for t in range(tiles):
        span = pl.ds(t * tile, tile)
        mixed = jnp.dot(table_in[span, :], basis[...], preferred_element_type=F32)
        across = t * tile + lax.broadcasted_iota(jnp.int32, (tile, width), 0)
        along = first[0] + lax.broadcasted_iota(jnp.int32, (tile, width), 1) // 2
        across_norm = jnp.minimum(across, rows - across).astype(F32) * (2.0 / rows)
        along_norm = jnp.minimum(along, length - along).astype(F32) * (2.0 / length)
        factor = 1.0 / (1.0 + across_norm * across_norm + along_norm * along_norm)
        for x in range(planes):
            cosine, sines = plane_phase(shifts[x], first[0], width, length)
            values = spec_in[x, span, :]
            phased = values * cosine + rotate(values) * sines
            out_from[x, span, :] = factor * (phased + mixed[:, x * width : (x + 1) * width])
        store = pltpu.make_async_copy(out_from.at[:, span, :], out.at[:, span, :], out_sems.at[t])
        store.start()
        stores.append(store)
    for store in stores:
        store.wait()


def back_rows(first, shifts, spread, turn, table, spec, length, unroll=16, tiles=4):
    planes, rows, width = spec.shape
    lanes_of = jnp.asarray(lane_table(width))
    small = pl.BlockSpec(memory_space=pltpu.SMEM)
    whole = pl.BlockSpec(memory_space=pltpu.VMEM)
    away = pl.BlockSpec(memory_space=pl.ANY)
    return pl.pallas_call(
        functools.partial(back_body, length, unroll, tiles),
        in_specs=[small, small, whole, whole, whole, away, away],
        out_specs=away,
        out_shape=jax.ShapeDtypeStruct((planes, rows, width), F32),
        scratch_shapes=[
            pltpu.VMEM((planes, rows, width), BF16),
            pltpu.VMEM((2 * rows, planes * width), BF16),
            pltpu.VMEM(table.shape, BF16),
            pltpu.VMEM(spec.shape, F32),
            pltpu.VMEM(spec.shape, F32),
            pltpu.SemaphoreType.DMA((2,)),
            pltpu.SemaphoreType.DMA((tiles,)),
        ],
        compiler_params=pltpu.CompilerParams(vmem_limit_bytes=VMEM_MIB * MIB),
        name="back_rows",
    )(first, shifts, spread, turn, lanes_of, table, spec)


def one_slab_on(value, by):
    size = lax.axis_size("slab")
    return lax.ppermute(value, "slab", [(i, i + by) for i in range(size) if 0 <= i + by < size])


def shards(spec_vel, shear_shift, patch_pos, patch_count, interp_w, marker_vel):
    planes, rows, width = spec_vel.shape
    pencils = lax.axis_size("pencil")
    own = rows // pencils
    length = width // 2 * pencils
    slots = patch_pos.shape[-1]
    first_wave = (lax.axis_index("pencil") * (width // 2)).astype(jnp.int32)
    first = first_wave[None]
    table = jnp.asarray(row_table(rows))

    positions = patch_pos[0, 0]
    coefs = forward_rows(first, shear_shift, spec_vel, table, own, length)
    later_wave, coefs = lax.optimization_barrier((first_wave, coefs))
    turn = spread_table(later_wave, width, length)
    positions, turn = lax.optimization_barrier((positions, turn))
    behind = one_slab_on(positions, 1)
    coefs = coefs.reshape(pencils, planes * own, width)
    here = lax.all_to_all(coefs, "pencil", split_axis=0, concat_axis=0, tiled=True)
    notes = []
    for held in (positions, behind):
        notes += [held[2] // 32, held[2] % 32, held[0] * own + held[1]]
    notes = jnp.stack(notes + [jnp.zeros_like(notes[0])] * 2).astype(BF16)

    spots = patch_spots(positions, behind, own)
    field, above = above_cells(spots, here, jnp.asarray(depth_table(length)), slots)
    from_above = one_slab_on(above, -1)
    values = own_cells(spots, field, slots)
    forces, spread, upward = marker_forces(
        patch_count[0], interp_w[0, 0], values, from_above, marker_vel[0, 0]
    )
    from_below = one_slab_on(upward, 1)
    message = jnp.concatenate([spread, from_below, notes])[None]
    gathered = lax.all_gather(message, "pencil", axis=0, tiled=True)
    new_hat = back_rows(first, shear_shift, gathered, turn, table, spec_vel, length)
    return (new_hat, forces[None, None])


def solution(mesh):
    placed = (
        P("slab", None, "pencil"),
        P("slab"),
        P("slab", "pencil", None, None),
        P("slab", "pencil"),
        P("slab", "pencil", None, None, None),
        P("slab", "pencil", None, None),
    )
    return jax.shard_map(
        shards,
        mesh=mesh,
        in_specs=placed,
        out_specs=(P("slab", None, "pencil"), P("slab", "pencil", None, None)),
        check_vma=False,
    )
```

```python
import functools
import math

import jax
import jax.numpy as jnp
import ml_dtypes
import numpy as np
from jax import lax
from jax.experimental import pallas as pl
from jax.experimental.pallas import tpu as pltpu
from jax.sharding import PartitionSpec as P

PD = 4
PZ = 16
MIB = 1 << 20
VMEM_MIB = 56
PITCH = 9
FIELD_TILES = 9
FIELD_PLANES = 15
F32 = jnp.float32
BF16 = jnp.bfloat16


def dft_tables(length):
    steps = np.arange(length, dtype=np.int64)
    turns = steps[:, None] * steps[None, :] % length
    angles = turns.astype(np.float32) * np.float32(2.0 * math.pi / length)
    norming = np.float32(1.0 / math.sqrt(length))
    return np.cos(angles) * norming, np.sin(angles) * norming


@functools.cache
def row_table(length):
    cosine, sines = dft_tables(length)
    return np.concatenate([cosine, sines], axis=1).astype(ml_dtypes.bfloat16)


@functools.cache
def depth_table(length):
    cosine, sines = dft_tables(length)
    merged = np.stack([cosine, -sines], axis=1).reshape(2 * length, length)
    return merged.astype(ml_dtypes.bfloat16)


def turn_cos_sin(turns):
    x = turns * math.pi
    x2 = x * x
    s = x * (
        1.0
        + x2
        * (
            -1.0 / 6
            + x2
            * (1.0 / 120 + x2 * (-1.0 / 5040 + x2 * (1.0 / 362880 + x2 * (-1.0 / 39916800))))
        )
    )
    c = 1.0 + x2 * (
        -0.5
        + x2
        * (1.0 / 24 + x2 * (-1.0 / 720 + x2 * (1.0 / 40320 + x2 * (-1.0 / 3628800))))
    )
    return 1.0 - 2.0 * s * s, 2.0 * s * c


def wave_turns(product, length):
    half = length // 2
    return (((product + half) & (length - 1)) - half).astype(F32) * (1.0 / length)


def rotate(values):
    width = values.shape[-1]
    lane = lax.broadcasted_iota(jnp.int32, values.shape, values.ndim - 1)
    axis = values.ndim - 1
    ahead = pltpu.roll(values, width - 1, axis)
    behind = pltpu.roll(values, 1, axis)
    return jnp.where(lane % 2 == 0, -ahead, behind)


def plane_phase(shift, first_wave, width, length):
    lane = lax.broadcasted_iota(jnp.int32, (1, width), 1)
    return turn_cos_sin(wave_turns((first_wave + lane // 2) * shift, length))


def forward_body(
    length, tiles, begin, first, shifts, spec, table, out,
    basis, spec_in, table_in, out_from, sems, table_sems, out_sems,
):
    planes, rows, width = spec_in.shape
    dests, _, own, _ = out_from.shape
    tile = rows // tiles
    loads = [
        pltpu.make_async_copy(spec.at[begin + x], spec_in.at[x], sems.at[x]) for x in range(planes)
    ]
    spans = [pl.ds(t * tile, tile) for t in range(tiles)]
    tables = [
        pltpu.make_async_copy(table.at[span, :], table_in.at[span, :], table_sems.at[t])
        for t, span in enumerate(spans)
    ]
    for load in loads + tables:
        load.start()
    for x in range(planes):
        loads[x].wait()
        cosine, sines = plane_phase(shifts[begin + x], first[0], width, length)
        values = spec_in[x]
        turned = rotate(values)
        lanes = pl.ds(x * width, width)
        basis[pl.ds(0, rows), lanes] = (values * cosine + turned * sines).astype(BF16)
        basis[pl.ds(rows, rows), lanes] = (turned * cosine - values * sines).astype(BF16)
    stores = []
    group = dests // tiles
    for t, span in enumerate(spans):
        tables[t].wait()
        mixed = jnp.dot(table_in[span, :], basis[...], preferred_element_type=F32).astype(BF16)
        for d in range(group):
            for x in range(planes):
                out_from[t * group + d, x] = mixed[
                    d * own : (d + 1) * own, x * width : (x + 1) * width
                ]
        ready = pl.ds(t * group, group)
        store = pltpu.make_async_copy(out_from.at[ready], out.at[ready], out_sems.at[t])
        store.start()
        stores.append(store)
    for store in stores:
        store.wait()


def forward_rows(first, shifts, spec, table, own, length, begin, planes, tiles=2):
    _, rows, width = spec.shape
    small = pl.BlockSpec(memory_space=pltpu.SMEM)
    away = pl.BlockSpec(memory_space=pl.ANY)
    shape = (rows // own, planes, own, width)
    return pl.pallas_call(
        functools.partial(forward_body, length, tiles, begin),
        in_specs=[small, small, away, away],
        out_specs=away,
        out_shape=jax.ShapeDtypeStruct(shape, BF16),
        scratch_shapes=[
            pltpu.VMEM((2 * rows, planes * width), BF16),
            pltpu.VMEM((planes, rows, width), F32),
            pltpu.VMEM(table.shape, BF16),
            pltpu.VMEM(shape, BF16),
            pltpu.SemaphoreType.DMA((planes,)),
            pltpu.SemaphoreType.DMA((tiles,)),
            pltpu.SemaphoreType.DMA((tiles,)),
        ],
        compiler_params=pltpu.CompilerParams(vmem_limit_bytes=VMEM_MIB * MIB),
        cost_estimate=pl.CostEstimate(
            flops=4 * rows * rows * planes * width,
            bytes_accessed=6 * planes * rows * width + 4 * rows * rows,
            transcendentals=0,
        ),
        name="forward_rows",
    )(first, shifts, spec, table)


def take_cells(spots, field, into, base, slots):
    lane = lax.broadcasted_iota(jnp.int32, (8, 128), 1)
    pitch = field.shape[0] // FIELD_TILES
    span = pitch // FIELD_PLANES
    batch = 16

    def body(i, carry):
        found = []
        for u in range(batch):
            spot = spots[base + i * batch + u]
            off = spots[base + slots + i * batch + u]
            near = field[pl.ds(spot, 8, stride=span), :]
            far = field[pl.ds(spot + pitch, 8, stride=span), :]
            found.append(pltpu.roll(jnp.where(lane >= off, near, far), 128 - off, 1))
        for u in range(batch):
            into[pl.ds((i * batch + u) * PITCH, 8), :] = found[u]
        return carry

    lax.fori_loop(0, slots // batch, body, 0)


def cells_first(into, slots):
    wide = lax.broadcasted_iota(jnp.int32, (slots, 128), 1) < PZ
    total = jnp.where(wide, into[pl.ds(0, slots, stride=PITCH), :], 0.0)
    for a in range(1, PD):
        part = jnp.where(wide, into[pl.ds(a, slots, stride=PITCH), :], 0.0)
        total += pltpu.roll(part, a * PZ, 1)
    return total.T


def above_body(slots, tiles, spots, lower, upper, table, field, above_out, into):
    sources, rows, width = lower.shape
    rows = 2 * rows
    own = rows // PD
    span = own + 1
    pitch = FIELD_PLANES * span
    blank = jnp.zeros((PD * span, 128), F32)
    for t in range(FIELD_TILES):
        field[pl.ds(t * pitch, PD * span), :] = blank
        field[pl.ds(t * pitch + 2 * PD * span, (PD - 1) * span), :] = blank[span:]
    field[pl.ds((FIELD_TILES - 1) * pitch + PD * span, PD * span), :] = blank
    left = jnp.concatenate(
        [
            jnp.concatenate([part[j] for j in range(sources)], axis=1)
            for part in (lower, upper)
        ],
        axis=0,
    )
    size = table.shape[1] // tiles
    parts = size // 128
    for t in range(tiles):
        velocity = jnp.dot(
            left, table[:, t * size : (t + 1) * size], preferred_element_type=F32
        )
        for j in range(parts):
            for x in range(PD):
                start = (parts * t + j) * pitch + (PD + x) * span
                field[pl.ds(start, own), :] = velocity[
                    x * own : (x + 1) * own, j * 128 : (j + 1) * 128
                ]
    take_cells(spots, field, into, 2 * slots, slots)
    above_out[...] = cells_first(into, slots)[PZ : PD * PZ]


def patch_spots(positions, behind, own):
    parts = []
    for held, lift in ((positions, PD), (behind, 0)):
        tile = held[2] // 128
        parts.append(
            (tile * FIELD_PLANES + held[0] + lift) * (own + 1) + held[1]
        )
        parts.append(held[2] % 128)
    return jnp.concatenate(parts)


def own_body(slots, pos, field, own_out, into):
    take_cells(pos, field, into, 0, slots)
    own_out[...] = cells_first(into, slots)[: PD * PZ]


def above_cells(spots, lower, upper, table, slots, tiles=2):
    rows = 2 * lower.shape[1]
    span = rows // PD + 1
    field_shape = (FIELD_TILES * FIELD_PLANES * span, 128)
    whole = pl.BlockSpec(memory_space=pltpu.VMEM)
    return pl.pallas_call(
        functools.partial(above_body, slots, tiles),
        in_specs=[pl.BlockSpec(memory_space=pltpu.SMEM), whole, whole, whole],
        out_specs=[whole, whole],
        out_shape=[
            jax.ShapeDtypeStruct(field_shape, F32),
            jax.ShapeDtypeStruct(((PD - 1) * PZ, slots), F32),
        ],
        scratch_shapes=[pltpu.VMEM((slots * PITCH, 128), F32)],
        compiler_params=pltpu.CompilerParams(vmem_limit_bytes=24 * MIB),
        name="above_cells",
    )(spots, lower, upper, table)


def own_cells(pos, field, slots):
    return pl.pallas_call(
        functools.partial(own_body, slots),
        in_specs=[
            pl.BlockSpec(memory_space=pltpu.SMEM),
            pl.BlockSpec(memory_space=pltpu.VMEM),
        ],
        out_specs=pl.BlockSpec(memory_space=pltpu.VMEM),
        out_shape=jax.ShapeDtypeStruct((PD * PZ, slots), F32),
        scratch_shapes=[pltpu.VMEM((slots * PITCH, 128), F32)],
        compiler_params=pltpu.CompilerParams(vmem_limit_bytes=24 * MIB),
        name="own_cells",
    )(pos, field)


def force_body(count, weights, own, above, target, forces, own_out, up_out, values, spread):
    step = pl.program_id(0)
    markers, cells, slots = weights.shape

    @pl.when(step == 0)
    def _():
        values[pl.ds(0, PZ), :] = own[pl.ds(0, PZ), :]
        values[pl.ds(PZ, cells - PZ), :] = own[pl.ds(PZ, cells - PZ), :] + above[...]
        spread[...] = jnp.zeros((cells, slots), F32)

    live = lax.broadcasted_iota(jnp.int32, (1, slots), 1) < count[0]
    held = values[...]
    total = spread[...]
    for m in range(markers):
        wide = weights[m].astype(F32)
        interp = jnp.sum(wide * held, axis=0, keepdims=True)
        force = jnp.where(live, target[pl.ds(m, 1), :] - interp, 0.0)
        forces[pl.ds(m, 1), :] = force
        total = total + wide * force
    spread[...] = total

    @pl.when(step == pl.num_programs(0) - 1)
    def _():
        own_out[...] = total.astype(BF16)
        up_out[...] = total[PZ:].astype(BF16)


def marker_forces(count, weights, own, above, target):
    markers, cells, slots = weights.shape
    steps = 4
    tile = markers // steps
    whole = lambda i: (0, 0)
    return pl.pallas_call(
        force_body,
        grid=(steps,),
        in_specs=[
            pl.BlockSpec(memory_space=pltpu.SMEM),
            pl.BlockSpec((tile, cells, slots), lambda i: (i, 0, 0)),
            pl.BlockSpec((cells, slots), whole),
            pl.BlockSpec((cells - PZ, slots), whole),
            pl.BlockSpec((tile, slots), lambda i: (i, 0)),
        ],
        out_specs=[
            pl.BlockSpec((tile, slots), lambda i: (i, 0)),
            pl.BlockSpec((cells, slots), whole),
            pl.BlockSpec((cells - PZ, slots), whole),
        ],
        out_shape=[
            jax.ShapeDtypeStruct((markers, slots), F32),
            jax.ShapeDtypeStruct((cells, slots), BF16),
            jax.ShapeDtypeStruct((cells - PZ, slots), BF16),
        ],
        scratch_shapes=[pltpu.VMEM((cells, slots), F32), pltpu.VMEM((cells, slots), F32)],
        compiler_params=pltpu.CompilerParams(vmem_limit_bytes=32 * MIB),
        name="marker_forces",
    )(count, weights, own, above, target)


def spread_table(first_wave, width, length):
    half = width // 2
    row = jnp.arange(width, dtype=jnp.int32)[:, None]
    cell = jnp.arange(PZ, dtype=jnp.int32)[None, :]
    wave = first_wave + row % half
    cosine, sines = turn_cos_sin(wave_turns(wave * cell, length))
    entry = jnp.where(row < half, cosine, -sines) * (1.0 / math.sqrt(length))
    high = entry.astype(BF16)
    low = (entry - high.astype(F32)).astype(BF16)
    blocks = 2 * PD - 1
    eye = jnp.eye(blocks, dtype=BF16)
    halves = [
        (eye[:, None, :, None] * part[None, :, None, :]).reshape(blocks * width, blocks * PZ)
        for part in (high, low)
    ]
    return jnp.concatenate(halves, axis=1)


def lane_table(width):
    half = width // 2
    table = np.zeros((width, 2 * width), np.float32)
    for k in range(half):
        table[k, 2 * k] = 1.0
        table[half + k, 2 * k + 1] = 1.0
        table[half + k, width + 2 * k] = 1.0
        table[k, width + 2 * k + 1] = -1.0
    return table.astype(ml_dtypes.bfloat16)


def merge_sources(length, first_wave, parts, turn, own, planes, width):
    half = width // 2
    cells = (2 * PD - 1) * PZ
    slots = parts[0].shape[1]
    wave = first_wave + lax.broadcasted_iota(jnp.int32, (half, 1), 0)
    place = lax.broadcasted_iota(jnp.int32, (slots, planes * own), 1).astype(F32)
    low_half = lax.broadcasted_iota(jnp.int32, (width, 128), 1) < own
    held = jnp.concatenate([part[:cells] for part in parts], axis=1)
    flat = jnp.dot(turn, jnp.concatenate([held, held], axis=0), preferred_element_type=F32)
    ready = []
    for u, part in enumerate(parts):
        notes = part[cells:].astype(F32)
        keys = notes.T
        mine = flat[:, u * slots : (u + 1) * slots]
        for side in range(2):
            start = notes[3 * side : 3 * side + 1] * 32.0 + notes[3 * side + 1 : 3 * side + 2]
            cosine, sines = turn_cos_sin(wave_turns(wave * start.astype(jnp.int32), length))
            hot = jnp.where(place == keys[:, 3 * side + 2 : 3 * side + 3], 1.0, 0.0)
            turned = []
            for block in range(PD) if side == 0 else range(PD, 2 * PD - 1):
                real = mine[block * width : block * width + half]
                imag = mine[block * width + half : (block + 1) * width]
                turned.append((real * cosine + imag * sines).astype(BF16))
                turned.append((imag * cosine - real * sines).astype(BF16))
            ready.append((jnp.concatenate(turned, axis=0), hot.astype(BF16)))
    landed = [jnp.dot(left, hot, preferred_element_type=F32) for left, hot in ready]
    kept = []
    for u in range(len(parts)):
        mine = [landed[2 * u][a * width : (a + 1) * width] for a in range(PD)]
        below = [None] + [landed[2 * u + 1][a * width : (a + 1) * width] for a in range(PD - 1)]
        one = [mine[1][:, :128], jnp.where(low_half, mine[1][:, 128:], below[1][:, 128:])]
        two = [mine[2][:, :128], below[2][:, 128:]]
        three = [jnp.where(low_half, mine[3][:, :128], below[3][:, :128]), below[3][:, 128:]]
        odd = [pltpu.roll(one[0] + three[1], own, 1), pltpu.roll(one[1] + three[0], own, 1)]
        near = mine[0][:, :128] + two[1] + jnp.where(low_half, odd[1], odd[0])
        far = mine[0][:, 128:] + two[0] + jnp.where(low_half, odd[0], odd[1])
        kept.append(jnp.concatenate([near.T, far.T], axis=0).astype(BF16))
    return kept


def back_body(
    length, unroll, tiles,
    first, shifts, spread, turn, lanes_of, table, spec, out,
    merged, basis, table_in, spec_in, out_from, sems, out_sems,
):
    planes, rows, width = spec_in.shape
    sources = spread.shape[0]
    own = rows // sources
    tile = rows // tiles
    loads = [
        pltpu.make_async_copy(table, table_in, sems.at[0]),
        pltpu.make_async_copy(spec, spec_in, sems.at[1]),
    ]
    for load in loads:
        load.start()

    def body(i, carry):
        parts = [spread[i * unroll + u] for u in range(unroll)]
        kept = merge_sources(length, first[0], parts, turn[...], own, planes, width)
        for u in range(unroll):
            base = pl.multiple_of((i * unroll + u) * own, own)
            for x in range(planes):
                merged[x, pl.ds(base, own), :] = kept[u][x * own : (x + 1) * own]
        return carry

    lax.fori_loop(0, sources // unroll, body, 0)
    for x in range(planes):
        spaced = jnp.dot(merged[x], lanes_of[...], preferred_element_type=F32).astype(BF16)
        into = pl.ds(x * width, width)
        basis[pl.ds(0, rows), into] = spaced[:, :width]
        basis[pl.ds(rows, rows), into] = spaced[:, width:]
    for load in loads:
        load.wait()
    stores = []
    for t in range(tiles):
        span = pl.ds(t * tile, tile)
        mixed = jnp.dot(table_in[span, :], basis[...], preferred_element_type=F32)
        across = t * tile + lax.broadcasted_iota(jnp.int32, (tile, width), 0)
        along = first[0] + lax.broadcasted_iota(jnp.int32, (tile, width), 1) // 2
        across_norm = jnp.minimum(across, rows - across).astype(F32) * (2.0 / rows)
        along_norm = jnp.minimum(along, length - along).astype(F32) * (2.0 / length)
        factor = 1.0 / (1.0 + across_norm * across_norm + along_norm * along_norm)
        for x in range(planes):
            cosine, sines = plane_phase(shifts[x], first[0], width, length)
            values = spec_in[x, span, :]
            phased = values * cosine + rotate(values) * sines
            out_from[x, span, :] = factor * (phased + mixed[:, x * width : (x + 1) * width])
        store = pltpu.make_async_copy(out_from.at[:, span, :], out.at[:, span, :], out_sems.at[t])
        store.start()
        stores.append(store)
    for store in stores:
        store.wait()


def back_rows(first, shifts, spread, turn, table, spec, length, unroll=16, tiles=4):
    planes, rows, width = spec.shape
    lanes_of = jnp.asarray(lane_table(width))
    small = pl.BlockSpec(memory_space=pltpu.SMEM)
    whole = pl.BlockSpec(memory_space=pltpu.VMEM)
    away = pl.BlockSpec(memory_space=pl.ANY)
    return pl.pallas_call(
        functools.partial(back_body, length, unroll, tiles),
        in_specs=[small, small, whole, whole, whole, away, away],
        out_specs=away,
        out_shape=jax.ShapeDtypeStruct((planes, rows, width), F32),
        scratch_shapes=[
            pltpu.VMEM((planes, rows, width), BF16),
            pltpu.VMEM((2 * rows, planes * width), BF16),
            pltpu.VMEM(table.shape, BF16),
            pltpu.VMEM(spec.shape, F32),
            pltpu.VMEM(spec.shape, F32),
            pltpu.SemaphoreType.DMA((2,)),
            pltpu.SemaphoreType.DMA((tiles,)),
        ],
        compiler_params=pltpu.CompilerParams(vmem_limit_bytes=VMEM_MIB * MIB),
        name="back_rows",
    )(first, shifts, spread, turn, lanes_of, table, spec)


def one_slab_on(value, by):
    size = lax.axis_size("slab")
    return lax.ppermute(value, "slab", [(i, i + by) for i in range(size) if 0 <= i + by < size])


def shards(spec_vel, shear_shift, patch_pos, patch_count, interp_w, marker_vel):
    planes, rows, width = spec_vel.shape
    pencils = lax.axis_size("pencil")
    own = rows // pencils
    length = width // 2 * pencils
    slots = patch_pos.shape[-1]
    first_wave = (lax.axis_index("pencil") * (width // 2)).astype(jnp.int32)
    first = first_wave[None]
    table = jnp.asarray(row_table(rows))

    positions = patch_pos[0, 0]
    half = planes // 2
    here = []
    wave = first
    for begin in (0, half):
        coefs = forward_rows(
            wave, shear_shift, spec_vel, table, own, length, begin, half
        ).reshape(pencils, half * own, width)
        wave, coefs = lax.optimization_barrier((wave, coefs))
        here.append(lax.all_to_all(coefs, "pencil", split_axis=0, concat_axis=0, tiled=True))
    later_wave = wave[0]
    turn = spread_table(later_wave, width, length)
    positions, turn = lax.optimization_barrier((positions, turn))
    behind = one_slab_on(positions, 1)
    notes = []
    for held in (positions, behind):
        notes += [held[2] // 32, held[2] % 32, held[0] * own + held[1]]
    notes = jnp.stack(notes + [jnp.zeros_like(notes[0])] * 2).astype(BF16)

    spots = patch_spots(positions, behind, own)
    field, above = above_cells(spots, here[0], here[1], jnp.asarray(depth_table(length)), slots)
    from_above = one_slab_on(above, -1)
    values = own_cells(spots, field, slots)
    forces, spread, upward = marker_forces(
        patch_count[0], interp_w[0, 0], values, from_above, marker_vel[0, 0]
    )
    from_below = one_slab_on(upward, 1)
    message = jnp.concatenate([spread, from_below, notes])[None]
    gathered = lax.all_gather(message, "pencil", axis=0, tiled=True)
    new_hat = back_rows(first, shear_shift, gathered, turn, table, spec_vel, length)
    return (new_hat, forces[None, None])


def solution(mesh):
    placed = (
        P("slab", None, "pencil"),
        P("slab"),
        P("slab", "pencil", None, None),
        P("slab", "pencil"),
        P("slab", "pencil", None, None, None),
        P("slab", "pencil", None, None),
    )
    return jax.shard_map(
        shards,
        mesh=mesh,
        in_specs=placed,
        out_specs=(P("slab", None, "pencil"), P("slab", "pencil", None, None)),
        check_vma=False,
    )
```

```python
import functools
import math

import jax
import jax.numpy as jnp
import ml_dtypes
import numpy as np
from jax import lax
from jax.experimental import pallas as pl
from jax.experimental.pallas import tpu as pltpu
from jax.sharding import PartitionSpec as P

PD = 4
PZ = 16
MIB = 1 << 20
VMEM_MIB = 56
PITCH = 9
FIELD_TILES = 9
FIELD_PLANES = 15
F32 = jnp.float32
BF16 = jnp.bfloat16


def dft_tables(length):
    steps = np.arange(length, dtype=np.int64)
    turns = steps[:, None] * steps[None, :] % length
    angles = turns.astype(np.float32) * np.float32(2.0 * math.pi / length)
    norming = np.float32(1.0 / math.sqrt(length))
    return np.cos(angles) * norming, np.sin(angles) * norming


@functools.cache
def row_table(length):
    cosine, sines = dft_tables(length)
    return np.concatenate([cosine, sines], axis=1).astype(ml_dtypes.bfloat16)


@functools.cache
def depth_table(length):
    cosine, sines = dft_tables(length)
    merged = np.stack([cosine, -sines], axis=1).reshape(2 * length, length)
    return merged.astype(ml_dtypes.bfloat16)


def turn_cos_sin(turns):
    x = turns * math.pi
    x2 = x * x
    s = x * (
        1.0
        + x2
        * (
            -1.0 / 6
            + x2
            * (1.0 / 120 + x2 * (-1.0 / 5040 + x2 * (1.0 / 362880 + x2 * (-1.0 / 39916800))))
        )
    )
    c = 1.0 + x2 * (
        -0.5
        + x2
        * (1.0 / 24 + x2 * (-1.0 / 720 + x2 * (1.0 / 40320 + x2 * (-1.0 / 3628800))))
    )
    return 1.0 - 2.0 * s * s, 2.0 * s * c


def wave_turns(product, length):
    half = length // 2
    return (((product + half) & (length - 1)) - half).astype(F32) * (1.0 / length)


def rotate(values):
    width = values.shape[-1]
    lane = lax.broadcasted_iota(jnp.int32, values.shape, values.ndim - 1)
    axis = values.ndim - 1
    ahead = pltpu.roll(values, width - 1, axis)
    behind = pltpu.roll(values, 1, axis)
    return jnp.where(lane % 2 == 0, -ahead, behind)


def plane_phase(shift, first_wave, width, length):
    lane = lax.broadcasted_iota(jnp.int32, (1, width), 1)
    return turn_cos_sin(wave_turns((first_wave + lane // 2) * shift, length))


def forward_body(
    length, tiles, first, shifts, spec, table, out,
    basis, spec_in, table_in, out_from, sems, table_sems, out_sems,
):
    planes, rows, width = spec_in.shape
    dests, _, own, _ = out_from.shape
    tile = rows // tiles
    loads = [pltpu.make_async_copy(spec.at[x], spec_in.at[x], sems.at[x]) for x in range(planes)]
    spans = [pl.ds(t * tile, tile) for t in range(tiles)]
    tables = [
        pltpu.make_async_copy(table.at[span, :], table_in.at[span, :], table_sems.at[t])
        for t, span in enumerate(spans)
    ]
    for load in loads + tables:
        load.start()
    for x in range(planes):
        loads[x].wait()
        cosine, sines = plane_phase(shifts[x], first[0], width, length)
        values = spec_in[x]
        turned = rotate(values)
        lanes = pl.ds(x * width, width)
        basis[pl.ds(0, rows), lanes] = (values * cosine + turned * sines).astype(BF16)
        basis[pl.ds(rows, rows), lanes] = (turned * cosine - values * sines).astype(BF16)
    stores = []
    group = dests // tiles
    for t, span in enumerate(spans):
        tables[t].wait()
        mixed = jnp.dot(table_in[span, :], basis[...], preferred_element_type=F32).astype(BF16)
        for d in range(group):
            for x in range(planes):
                out_from[t * group + d, x] = mixed[
                    d * own : (d + 1) * own, x * width : (x + 1) * width
                ]
        ready = pl.ds(t * group, group)
        store = pltpu.make_async_copy(out_from.at[ready], out.at[ready], out_sems.at[t])
        store.start()
        stores.append(store)
    for store in stores:
        store.wait()


def forward_rows(first, shifts, spec, table, own, length, tiles=2):
    planes, rows, width = spec.shape
    small = pl.BlockSpec(memory_space=pltpu.SMEM)
    away = pl.BlockSpec(memory_space=pl.ANY)
    shape = (rows // own, planes, own, width)
    return pl.pallas_call(
        functools.partial(forward_body, length, tiles),
        in_specs=[small, small, away, away],
        out_specs=away,
        out_shape=jax.ShapeDtypeStruct(shape, BF16),
        scratch_shapes=[
            pltpu.VMEM((2 * rows, planes * width), BF16),
            pltpu.VMEM(spec.shape, F32),
            pltpu.VMEM(table.shape, BF16),
            pltpu.VMEM(shape, BF16),
            pltpu.SemaphoreType.DMA((planes,)),
            pltpu.SemaphoreType.DMA((tiles,)),
            pltpu.SemaphoreType.DMA((tiles,)),
        ],
        compiler_params=pltpu.CompilerParams(vmem_limit_bytes=VMEM_MIB * MIB),
        name="forward_rows",
    )(first, shifts, spec, table)


def take_cells(spots, field, into, base, slots):
    lane = lax.broadcasted_iota(jnp.int32, (8, 128), 1)
    pitch = field.shape[0] // FIELD_TILES
    span = pitch // FIELD_PLANES
    batch = 16

    def body(i, carry):
        found = []
        for u in range(batch):
            spot = spots[base + i * batch + u]
            off = spots[base + slots + i * batch + u]
            near = field[pl.ds(spot, 8, stride=span), :]
            far = field[pl.ds(spot + pitch, 8, stride=span), :]
            found.append(pltpu.roll(jnp.where(lane >= off, near, far), 128 - off, 1))
        for u in range(batch):
            into[pl.ds((i * batch + u) * PITCH, 8), :] = found[u]
        return carry

    lax.fori_loop(0, slots // batch, body, 0)


def cells_first(into, slots):
    wide = lax.broadcasted_iota(jnp.int32, (slots, 128), 1) < PZ
    total = jnp.where(wide, into[pl.ds(0, slots, stride=PITCH), :], 0.0)
    for a in range(1, PD):
        part = jnp.where(wide, into[pl.ds(a, slots, stride=PITCH), :], 0.0)
        total += pltpu.roll(part, a * PZ, 1)
    return total.T


def above_body(slots, tiles, spots, coefs, table, field, above_out, into):
    sources, rows, width = coefs.shape
    own = rows // PD
    span = own + 1
    pitch = FIELD_PLANES * span
    blank = jnp.zeros((PD * span, 128), F32)
    for t in range(FIELD_TILES):
        field[pl.ds(t * pitch, PD * span), :] = blank
        field[pl.ds(t * pitch + 2 * PD * span, (PD - 1) * span), :] = blank[span:]
    field[pl.ds((FIELD_TILES - 1) * pitch + PD * span, PD * span), :] = blank
    left = jnp.concatenate([coefs[j] for j in range(sources)], axis=1)
    size = table.shape[1] // tiles
    parts = size // 128
    for t in range(tiles):
        velocity = jnp.dot(
            left, table[:, t * size : (t + 1) * size], preferred_element_type=F32
        )
        for j in range(parts):
            for x in range(PD):
                start = (parts * t + j) * pitch + (PD + x) * span
                field[pl.ds(start, own), :] = velocity[
                    x * own : (x + 1) * own, j * 128 : (j + 1) * 128
                ]
    take_cells(spots, field, into, 2 * slots, slots)
    above_out[...] = cells_first(into, slots)[PZ : PD * PZ]


def patch_spots(positions, behind, own):
    parts = []
    for held, lift in ((positions, PD), (behind, 0)):
        tile = held[2] // 128
        parts.append(
            (tile * FIELD_PLANES + held[0] + lift) * (own + 1) + held[1]
        )
        parts.append(held[2] % 128)
    return jnp.concatenate(parts)


def own_body(slots, pos, field, own_out, into):
    take_cells(pos, field, into, 0, slots)
    own_out[...] = cells_first(into, slots)[: PD * PZ]


def above_cells(spots, coefs, table, slots, tiles=2):
    rows = coefs.shape[1]
    span = rows // PD + 1
    field_shape = (FIELD_TILES * FIELD_PLANES * span, 128)
    whole = pl.BlockSpec(memory_space=pltpu.VMEM)
    return pl.pallas_call(
        functools.partial(above_body, slots, tiles),
        in_specs=[pl.BlockSpec(memory_space=pltpu.SMEM), whole, whole],
        out_specs=[whole, whole],
        out_shape=[
            jax.ShapeDtypeStruct(field_shape, F32),
            jax.ShapeDtypeStruct(((PD - 1) * PZ, slots), F32),
        ],
        scratch_shapes=[pltpu.VMEM((slots * PITCH, 128), F32)],
        compiler_params=pltpu.CompilerParams(vmem_limit_bytes=24 * MIB),
        name="above_cells",
    )(spots, coefs, table)


def own_cells(pos, field, slots):
    return pl.pallas_call(
        functools.partial(own_body, slots),
        in_specs=[
            pl.BlockSpec(memory_space=pltpu.SMEM),
            pl.BlockSpec(memory_space=pltpu.VMEM),
        ],
        out_specs=pl.BlockSpec(memory_space=pltpu.VMEM),
        out_shape=jax.ShapeDtypeStruct((PD * PZ, slots), F32),
        scratch_shapes=[pltpu.VMEM((slots * PITCH, 128), F32)],
        compiler_params=pltpu.CompilerParams(vmem_limit_bytes=24 * MIB),
        name="own_cells",
    )(pos, field)


def force_body(count, weights, own, above, target, forces, own_out, up_out, values, spread):
    step = pl.program_id(0)
    markers, cells, slots = weights.shape

    @pl.when(step == 0)
    def _():
        values[pl.ds(0, PZ), :] = own[pl.ds(0, PZ), :]
        values[pl.ds(PZ, cells - PZ), :] = own[pl.ds(PZ, cells - PZ), :] + above[...]
        spread[...] = jnp.zeros((cells, slots), F32)

    live = lax.broadcasted_iota(jnp.int32, (1, slots), 1) < count[0]
    held = values[...]
    total = spread[...]
    for m in range(markers):
        wide = weights[m].astype(F32)
        interp = jnp.sum(wide * held, axis=0, keepdims=True)
        force = jnp.where(live, target[pl.ds(m, 1), :] - interp, 0.0)
        forces[pl.ds(m, 1), :] = force
        total = total + wide * force
    spread[...] = total

    @pl.when(step == pl.num_programs(0) - 1)
    def _():
        own_out[...] = total.astype(BF16)
        up_out[...] = total[PZ:].astype(BF16)


def marker_forces(count, weights, own, above, target):
    markers, cells, slots = weights.shape
    steps = 2
    tile = markers // steps
    whole = lambda i: (0, 0)
    return pl.pallas_call(
        force_body,
        grid=(steps,),
        in_specs=[
            pl.BlockSpec(memory_space=pltpu.SMEM),
            pl.BlockSpec((tile, cells, slots), lambda i: (i, 0, 0)),
            pl.BlockSpec((cells, slots), whole),
            pl.BlockSpec((cells - PZ, slots), whole),
            pl.BlockSpec((tile, slots), lambda i: (i, 0)),
        ],
        out_specs=[
            pl.BlockSpec((tile, slots), lambda i: (i, 0)),
            pl.BlockSpec((cells, slots), whole),
            pl.BlockSpec((cells - PZ, slots), whole),
        ],
        out_shape=[
            jax.ShapeDtypeStruct((markers, slots), F32),
            jax.ShapeDtypeStruct((cells, slots), BF16),
            jax.ShapeDtypeStruct((cells - PZ, slots), BF16),
        ],
        scratch_shapes=[pltpu.VMEM((cells, slots), F32), pltpu.VMEM((cells, slots), F32)],
        compiler_params=pltpu.CompilerParams(vmem_limit_bytes=32 * MIB),
        name="marker_forces",
    )(count, weights, own, above, target)


def spread_table(first_wave, width, length):
    half = width // 2
    row = jnp.arange(width, dtype=jnp.int32)[:, None]
    cell = jnp.arange(PZ, dtype=jnp.int32)[None, :]
    wave = first_wave + row % half
    cosine, sines = turn_cos_sin(wave_turns(wave * cell, length))
    entry = jnp.where(row < half, cosine, -sines) * (1.0 / math.sqrt(length))
    high = entry.astype(BF16)
    low = (entry - high.astype(F32)).astype(BF16)
    blocks = 2 * PD - 1
    eye = jnp.eye(blocks, dtype=BF16)
    halves = [
        (eye[:, None, :, None] * part[None, :, None, :]).reshape(blocks * width, blocks * PZ)
        for part in (high, low)
    ]
    return jnp.concatenate(halves, axis=1)


def lane_table(width):
    half = width // 2
    table = np.zeros((width, 2 * width), np.float32)
    for k in range(half):
        table[k, 2 * k] = 1.0
        table[half + k, 2 * k + 1] = 1.0
        table[half + k, width + 2 * k] = 1.0
        table[k, width + 2 * k + 1] = -1.0
    return table.astype(ml_dtypes.bfloat16)


def merge_sources(length, first_wave, parts, turn, own, planes, width):
    half = width // 2
    cells = (2 * PD - 1) * PZ
    slots = parts[0].shape[1]
    wave = first_wave + lax.broadcasted_iota(jnp.int32, (half, 1), 0)
    place = lax.broadcasted_iota(jnp.int32, (slots, planes * own), 1).astype(F32)
    low_half = lax.broadcasted_iota(jnp.int32, (width, 128), 1) < own
    held = jnp.concatenate([part[:cells] for part in parts], axis=1)
    flat = jnp.dot(turn, jnp.concatenate([held, held], axis=0), preferred_element_type=F32)
    ready = []
    for u, part in enumerate(parts):
        notes = part[cells:].astype(F32)
        keys = notes.T
        mine = flat[:, u * slots : (u + 1) * slots]
        for side in range(2):
            start = notes[3 * side : 3 * side + 1] * 32.0 + notes[3 * side + 1 : 3 * side + 2]
            cosine, sines = turn_cos_sin(wave_turns(wave * start.astype(jnp.int32), length))
            hot = jnp.where(place == keys[:, 3 * side + 2 : 3 * side + 3], 1.0, 0.0)
            turned = []
            for block in range(PD) if side == 0 else range(PD, 2 * PD - 1):
                real = mine[block * width : block * width + half]
                imag = mine[block * width + half : (block + 1) * width]
                turned.append((real * cosine + imag * sines).astype(BF16))
                turned.append((imag * cosine - real * sines).astype(BF16))
            ready.append((jnp.concatenate(turned, axis=0), hot.astype(BF16)))
    landed = [jnp.dot(left, hot, preferred_element_type=F32) for left, hot in ready]
    kept = []
    for u in range(len(parts)):
        mine = [landed[2 * u][a * width : (a + 1) * width] for a in range(PD)]
        below = [None] + [landed[2 * u + 1][a * width : (a + 1) * width] for a in range(PD - 1)]
        one = [mine[1][:, :128], jnp.where(low_half, mine[1][:, 128:], below[1][:, 128:])]
        two = [mine[2][:, :128], below[2][:, 128:]]
        three = [jnp.where(low_half, mine[3][:, :128], below[3][:, :128]), below[3][:, 128:]]
        odd = [pltpu.roll(one[0] + three[1], own, 1), pltpu.roll(one[1] + three[0], own, 1)]
        near = mine[0][:, :128] + two[1] + jnp.where(low_half, odd[1], odd[0])
        far = mine[0][:, 128:] + two[0] + jnp.where(low_half, odd[0], odd[1])
        kept.append(jnp.concatenate([near.T, far.T], axis=0).astype(BF16))
    return kept


def back_body(
    length, unroll, tiles,
    first, shifts, spread, turn, lanes_of, table, spec, out,
    merged, basis, table_in, spec_in, out_from, sems, out_sems,
):
    planes, rows, width = spec_in.shape
    sources = spread.shape[0]
    own = rows // sources
    tile = rows // tiles
    loads = [
        pltpu.make_async_copy(table, table_in, sems.at[0]),
        pltpu.make_async_copy(spec, spec_in, sems.at[1]),
    ]
    for load in loads:
        load.start()

    def body(i, carry):
        parts = [spread[i * unroll + u] for u in range(unroll)]
        kept = merge_sources(length, first[0], parts, turn[...], own, planes, width)
        for u in range(unroll):
            base = pl.multiple_of((i * unroll + u) * own, own)
            for x in range(planes):
                merged[x, pl.ds(base, own), :] = kept[u][x * own : (x + 1) * own]
        return carry

    lax.fori_loop(0, sources // unroll, body, 0)
    for x in range(planes):
        spaced = jnp.dot(merged[x], lanes_of[...], preferred_element_type=F32).astype(BF16)
        into = pl.ds(x * width, width)
        basis[pl.ds(0, rows), into] = spaced[:, :width]
        basis[pl.ds(rows, rows), into] = spaced[:, width:]
    for load in loads:
        load.wait()
    stores = []
    for t in range(tiles):
        span = pl.ds(t * tile, tile)
        mixed = jnp.dot(table_in[span, :], basis[...], preferred_element_type=F32)
        across = t * tile + lax.broadcasted_iota(jnp.int32, (tile, width), 0)
        along = first[0] + lax.broadcasted_iota(jnp.int32, (tile, width), 1) // 2
        across_norm = jnp.minimum(across, rows - across).astype(F32) * (2.0 / rows)
        along_norm = jnp.minimum(along, length - along).astype(F32) * (2.0 / length)
        factor = 1.0 / (1.0 + across_norm * across_norm + along_norm * along_norm)
        for x in range(planes):
            cosine, sines = plane_phase(shifts[x], first[0], width, length)
            values = spec_in[x, span, :]
            phased = values * cosine + rotate(values) * sines
            out_from[x, span, :] = factor * (phased + mixed[:, x * width : (x + 1) * width])
        store = pltpu.make_async_copy(out_from.at[:, span, :], out.at[:, span, :], out_sems.at[t])
        store.start()
        stores.append(store)
    for store in stores:
        store.wait()


def back_rows(first, shifts, spread, turn, table, spec, length, unroll=16, tiles=4):
    planes, rows, width = spec.shape
    lanes_of = jnp.asarray(lane_table(width))
    small = pl.BlockSpec(memory_space=pltpu.SMEM)
    whole = pl.BlockSpec(memory_space=pltpu.VMEM)
    away = pl.BlockSpec(memory_space=pl.ANY)
    return pl.pallas_call(
        functools.partial(back_body, length, unroll, tiles),
        in_specs=[small, small, whole, whole, whole, away, away],
        out_specs=away,
        out_shape=jax.ShapeDtypeStruct((planes, rows, width), F32),
        scratch_shapes=[
            pltpu.VMEM((planes, rows, width), BF16),
            pltpu.VMEM((2 * rows, planes * width), BF16),
            pltpu.VMEM(table.shape, BF16),
            pltpu.VMEM(spec.shape, F32),
            pltpu.VMEM(spec.shape, F32),
            pltpu.SemaphoreType.DMA((2,)),
            pltpu.SemaphoreType.DMA((tiles,)),
        ],
        compiler_params=pltpu.CompilerParams(vmem_limit_bytes=VMEM_MIB * MIB),
        name="back_rows",
    )(first, shifts, spread, turn, lanes_of, table, spec)


def one_slab_on(value, by):
    size = lax.axis_size("slab")
    return lax.ppermute(value, "slab", [(i, i + by) for i in range(size) if 0 <= i + by < size])


def shards(spec_vel, shear_shift, patch_pos, patch_count, interp_w, marker_vel):
    planes, rows, width = spec_vel.shape
    pencils = lax.axis_size("pencil")
    own = rows // pencils
    length = width // 2 * pencils
    slots = patch_pos.shape[-1]
    first_wave = (lax.axis_index("pencil") * (width // 2)).astype(jnp.int32)
    first = first_wave[None]
    table = jnp.asarray(row_table(rows))

    positions = patch_pos[0, 0]
    coefs = forward_rows(first, shear_shift, spec_vel, table, own, length)
    later_wave, coefs = lax.optimization_barrier((first_wave, coefs))
    turn = spread_table(later_wave, width, length)
    positions, turn = lax.optimization_barrier((positions, turn))
    behind = one_slab_on(positions, 1)
    coefs = coefs.reshape(pencils, planes * own, width)
    here = lax.all_to_all(coefs, "pencil", split_axis=0, concat_axis=0, tiled=True)
    notes = []
    for held in (positions, behind):
        notes += [held[2] // 32, held[2] % 32, held[0] * own + held[1]]
    notes = jnp.stack(notes + [jnp.zeros_like(notes[0])] * 2).astype(BF16)

    spots = patch_spots(positions, behind, own)
    field, above = above_cells(spots, here, jnp.asarray(depth_table(length)), slots)
    from_above = one_slab_on(above, -1)
    values = own_cells(spots, field, slots)
    forces, spread, upward = marker_forces(
        patch_count[0], interp_w[0, 0], values, from_above, marker_vel[0, 0]
    )
    from_below = one_slab_on(upward, 1)
    message = jnp.concatenate([spread, from_below, notes])[None]
    gathered = lax.all_gather(message, "pencil", axis=0, tiled=True)
    new_hat = back_rows(first, shear_shift, gathered, turn, table, spec_vel, length)
    return (new_hat, forces[None, None])


def solution(mesh):
    placed = (
        P("slab", None, "pencil"),
        P("slab"),
        P("slab", "pencil", None, None),
        P("slab", "pencil"),
        P("slab", "pencil", None, None, None),
        P("slab", "pencil", None, None),
    )
    return jax.shard_map(
        shards,
        mesh=mesh,
        in_specs=placed,
        out_specs=(P("slab", None, "pencil"), P("slab", "pencil", None, None)),
        check_vma=False,
    )
```
